32 devices in a mesh: slot: 8 (over y, x, core), replica: 4 (over z).
Axes of the slice: x: 2, y: 2, z: 4, core: 2. Of those that a mesh axis runs over, the one named last changes fastest.
Arguments:
- layer_in: bfloat16 [4, 2432, 2560], P('replica', 'slot'), may hold values from -36 to 36
- seg_starts: int32 [4, 13], P('replica'), may hold values from 0 to 2304, as said below
- seg_parents: int32 [4, 13], P('replica'), may hold values from 0 to 4, as said below
- w_query: bfloat16 [2560, 2560], P('slot'), may hold values from -0.125 to 0.125
- w_key: bfloat16 [2560, 640], P('slot'), may hold values from -0.125 to 0.125
- w_value: bfloat16 [2560, 640], P('slot'), may hold values from -0.125 to 0.125
- w_out: bfloat16 [2560, 2560], P('slot'), may hold values from -2 to 2
- w_gate: bfloat16 [2560, 6912], P('slot'), may hold values from -0.125 to 0.125
- w_up: bfloat16 [2560, 6912], P('slot'), may hold values from -0.125 to 0.125
- w_down: bfloat16 [6912, 2560], P('slot'), may hold values from -0.078125 to 0.078125
- gain_attn: bfloat16 [2560], P('slot'), may hold values from 0.5 to 1.5
- gain_ffn: bfloat16 [2560], P('slot'), may hold values from 0.5 to 1.5
- out_cotangent: bfloat16 [4, 2432, 2560], P('replica', 'slot'), may hold values from -6 to 6
Outputs:
- layer_out: bfloat16 [4, 2432, 2560], P('replica', 'slot')
- grad_in: bfloat16 [4, 2432, 2560], P('replica', 'slot')
- grad_query: float32 [2560, 2560], P('slot')
- grad_key: float32 [2560, 640], P('slot')
- grad_value: float32 [2560, 640], P('slot')
- grad_proj: float32 [2560, 2560], P('slot')
- grad_gate: float32 [2560, 6912], P('slot')
- grad_up: float32 [2560, 6912], P('slot')
- grad_down: float32 [6912, 2560], P('slot')
- grad_gain_attn: float32 [2560], P('slot')
- grad_gain_ffn: float32 [2560], P('slot')
The draws below stay inside these ranges and needn't reach their ends.
Inputs may be any that keep to these rules, and one draw needn't show every extreme that they name: `seg_starts`: segments of one tree never intersect; the trunk starts at slot 0 and some segment ends at slot 2431. `seg_parents`: the trunk's and every branch's entry is 0; each leaf's entry is a branch, and each branch is the parent of 2 leaves.
All inputs are finite; a program needn't handle non-finite values.
Results may differ from the reference program's by a relative error of at most 0.023.
Values may be sent and summed in bfloat16 or wider, within the bound.
No kernel may reach another device: no remote copies, remote signals or barrier semaphores. Data moves between devices by JAX's collectives and lax.ppermute only.
A program may use at most 576 MiB of HBM per device.

```python
import math
import jax
import jax.numpy as jnp
from jax import lax

D = 2560
HEADS = 32
KV_HEADS = 8
HEAD_DIM = 80
FF = 6912
TRUNK = 768
BRANCH = 128
LEAF = 128
NBRANCH = 4
NLEAF = 8
PAD = 128
QDIM = 2560
KVDIM = 640
SEGS = 13
SLOTS = 2432
TREES = 4


def layout_starts(key):
    order_key, gap_key = jax.random.split(key)
    others = jax.random.permutation(order_key, SEGS - 1).astype(jnp.int32) + 1
    order = jnp.concatenate([jnp.zeros((1,), jnp.int32), others])
    lengths = jnp.where(order == 0, TRUNK, jnp.where(order <= NBRANCH, BRANCH, LEAF)).astype(jnp.int32)
    cuts = jnp.sort(jax.random.permutation(gap_key, PAD + SEGS - 2)[:SEGS - 2]).astype(jnp.int32)
    edges = jnp.concatenate([jnp.full((1,), -1, jnp.int32), cuts, jnp.full((1,), PAD + SEGS - 2, jnp.int32)])
    gaps = edges[1:] - edges[:-1] - 1
    placed = jnp.concatenate([jnp.zeros((1,), jnp.int32), jnp.cumsum(lengths[:-1] + gaps).astype(jnp.int32)])
    return placed[jnp.argsort(order)]


def draw_seg_starts(key, part):
    key = jax.random.fold_in(key, 5)
    return jax.vmap(layout_starts)(jax.random.split(key, TREES)).astype(jnp.int32)


def leaf_parents(key):
    leaves = 1 + jax.random.permutation(key, NLEAF).astype(jnp.int32) // (NLEAF // NBRANCH)
    return jnp.concatenate([jnp.zeros((1 + NBRANCH,), jnp.int32), leaves])


def draw_seg_parents(key, part):
    key = jax.random.fold_in(key, 7)
    return jax.vmap(leaf_parents)(jax.random.split(key, TREES)).astype(jnp.int32)


def draw_layer_in(key, part):
    key = jax.random.fold_in(key, 3)
    row_key, col_key, base_key = jax.random.split(key, 3)
    row_scale = jnp.exp(jax.random.uniform(row_key, (TREES, SLOTS, 1), jnp.float32, math.log(0.3), math.log(3.0)))
    col_scale = jnp.exp(jax.random.uniform(col_key, (1, 1, D), jnp.float32, math.log(0.3), math.log(3.0)))
    base = jax.random.truncated_normal(base_key, -4.0, 4.0, (TREES, SLOTS, D), jnp.float32)
    return (base * row_scale * col_scale).astype(jnp.bfloat16)


def levels(stream_key, dims, cuts, least, top_value):
    factor_of = 1.0
    for dim, parts in cuts:
        draws = jax.random.uniform(jax.random.fold_in(jax.random.fold_in(stream_key, 6), dim), (parts,), jnp.float32, least / len(cuts), top_value / len(cuts))
        factor_of = factor_of * jnp.repeat(jnp.exp(draws), dims[dim] // parts).reshape((-1,) + (1,) * (len(dims) - 1 - dim))
    return factor_of


def normal_values(stream_key, dims, spread, bound, cuts=(), kind=jnp.bfloat16):
    array = jax.random.normal(stream_key, dims, jnp.float32) * spread
    if len(cuts) > 0:
        array = levels(stream_key, dims, cuts, -0.22, 0.18) * array
    return jnp.clip(array, min=-bound, max=bound).astype(kind)


def setup_inputs(seed: int = 0) -> dict:
    splits = jax.random.split(jax.random.key(seed), 14)
    layer_in = draw_layer_in(jax.random.fold_in(splits[13], 71), 0)
    seg_starts = draw_seg_starts(jax.random.fold_in(splits[13], 71), 0)
    seg_parents = draw_seg_parents(jax.random.fold_in(splits[13], 71), 0)
    w_query = normal_values(splits[3], (D, QDIM), D ** -0.5, 0.125, ((0, 8),))
    w_key = normal_values(splits[4], (D, KVDIM), D ** -0.5, 0.125, ((0, 8),))
    w_value = normal_values(splits[5], (D, KVDIM), D ** -0.5, 0.125, ((0, 8),))
    w_out = normal_values(splits[6], (QDIM, D), (max(D // 256, 1)) ** -0.5, 2.0, ((0, 8),))
    w_gate = normal_values(splits[7], (D, FF), D ** -0.5, 0.125, ((0, 8),))
    w_up = normal_values(splits[8], (D, FF), D ** -0.5, 0.125, ((0, 8),))
    w_down = normal_values(splits[9], (FF, D), FF ** -0.5, 0.078125, ((0, 8),))
    gain_attn = jnp.clip(1.0 + 0.1 * jax.random.normal(splits[10], (D,), jnp.float32), 0.5, 1.5).astype(jnp.bfloat16)
    gain_ffn = jnp.clip(1.0 + 0.1 * jax.random.normal(splits[11], (D,), jnp.float32), 0.5, 1.5).astype(jnp.bfloat16)
    out_cotangent = normal_values(splits[12], (TREES, SLOTS, D), 1.0, 6.0, ((0, 4), (1, 8)))
    return {"layer_in": layer_in, "seg_starts": seg_starts, "seg_parents": seg_parents, "w_query": w_query, "w_key": w_key, "w_value": w_value, "w_out": w_out, "w_gate": w_gate, "w_up": w_up, "w_down": w_down, "gain_attn": gain_attn, "gain_ffn": gain_ffn, "out_cotangent": out_cotangent}


epsilon = 1e-05
rope_theta = 10000.0
masked_score = -1e+30
highest = lax.Precision.HIGHEST

@jax.custom_vjp
def low(v):
    return lax.optimization_barrier(v.astype(jnp.bfloat16)).astype(jnp.float32)

@jax.custom_vjp
def low_back(v):
    return v

def low_keep(v):
    return (low(v), None)

def low_pass(kept, grad):
    return (grad,)

def back_keep(v):
    return (v, None)

def back_low(kept, grad):
    return (low(grad),)
low.defvjp(low_keep, low_pass)
low_back.defvjp(back_keep, back_low)

def matmul_hi(left, right):
    return jnp.dot(left, right, precision=highest, preferred_element_type=jnp.float32)

def rms_unit(values):
    return values * lax.rsqrt(lax.optimization_barrier(jnp.mean(values * values, axis=-1, keepdims=True)) + epsilon)

def rotate(values, position):
    half_dim = HEAD_DIM // 2
    frequency = jnp.power(rope_theta, -2.0 * jnp.arange(half_dim).astype(jnp.float32) / HEAD_DIM)
    angle = position.astype(jnp.float32)[:, None] * frequency[None, :]
    cosine = jnp.cos(angle)[:, None, :]
    sine = jnp.sin(angle)[:, None, :]
    former = values[..., :half_dim]
    latter = values[..., half_dim:]
    return jnp.concatenate([former * cosine - latter * sine, latter * cosine + former * sine], axis=-1)

def layout(starts, parents):
    segment_ids = jnp.arange(SEGS, dtype=jnp.int32)
    segment_len = jnp.where(segment_ids == 0, TRUNK, jnp.where(segment_ids <= NBRANCH, BRANCH, LEAF)).astype(jnp.int32)
    depth_base = jnp.where(segment_ids == 0, 0, jnp.where(segment_ids <= NBRANCH, TRUNK, TRUNK + BRANCH)).astype(jnp.int32)
    slot_index = jnp.arange(SLOTS, dtype=jnp.int32)
    inside = (slot_index[None, :] >= starts[:, None]) & (slot_index[None, :] < (starts + segment_len)[:, None])
    live_slot = jnp.any(inside, axis=0)
    segment = (lax.optimization_barrier(jnp.sum(jnp.where(inside, segment_ids[:, None], 0), axis=0)) + jnp.where(live_slot, 0, SEGS)).astype(jnp.int32)
    position = lax.optimization_barrier(jnp.sum(jnp.where(inside, slot_index[None, :] - starts[:, None] + depth_base[:, None], 0), axis=0)).astype(jnp.int32)
    grandparent = parents[parents]
    ancestry = (segment_ids[:, None] == segment_ids[None, :]) | (parents[:, None] == segment_ids[None, :]) | (grandparent[:, None] == segment_ids[None, :])
    ancestry = jnp.pad(ancestry, ((0, 1), (0, 1)))
    return (position, ancestry, segment, live_slot)

def tree_forward(inputs, weight_set, position, ancestry, segment):
    w_query, w_key, w_value, w_out, w_gate, w_up, w_down, gain_attn, gain_ffn = weight_set
    head_group = HEADS // KV_HEADS
    attn_input = low(rms_unit(inputs) * gain_attn)
    query_pre = low_back(matmul_hi(attn_input, w_query))
    key_pre = low_back(matmul_hi(attn_input, w_key))
    values = low(low_back(matmul_hi(attn_input, w_value))).reshape(SLOTS, KV_HEADS, HEAD_DIM)
    queries = low(rotate(query_pre.reshape(SLOTS, HEADS, HEAD_DIM), position)).reshape(SLOTS, KV_HEADS, head_group, HEAD_DIM)
    keys = low(rotate(key_pre.reshape(SLOTS, KV_HEADS, HEAD_DIM), position))
    slot_index = jnp.arange(SLOTS, dtype=jnp.int32)
    block_len = SLOTS // 4

    def attend(block_items):
        query_block, query_slot, query_pos, query_seg = block_items
        logits = low_back(jnp.einsum('qkgd,tkd->kgqt', query_block, keys, precision=highest) * HEAD_DIM ** (-0.5))
        permitted = (query_slot[:, None] == slot_index[None, :]) | ancestry[query_seg[:, None], segment[None, :]] & (position[None, :] <= query_pos[:, None])
        masked = jnp.where(permitted, logits, masked_score)
        log_total = jax.nn.logsumexp(masked, axis=-1, keepdims=True)
        probs = low(jnp.exp(masked - log_total))
        return jnp.einsum('kgqt,tkd->qkgd', probs, values, precision=highest)
    blocks = (queries.reshape(4, block_len, KV_HEADS, head_group, HEAD_DIM), slot_index.reshape(4, block_len), position.reshape(4, block_len), segment.reshape(4, block_len))
    attended = lax.map(jax.checkpoint(attend), blocks).reshape(SLOTS, HEADS * HEAD_DIM)
    attended = low_back(low(attended))
    middle = inputs + low_back(matmul_hi(attended, w_out))
    ffn_input = low(rms_unit(middle) * gain_ffn)
    gate_proj = low_back(matmul_hi(ffn_input, w_gate))
    up_proj = low_back(matmul_hi(ffn_input, w_up))
    activated = low(jax.nn.silu(gate_proj) * up_proj)
    return middle + low_back(matmul_hi(activated, w_down))

def reference(layer_in, seg_starts, seg_parents, w_query, w_key, w_value, w_out, w_gate, w_up, w_down, gain_attn, gain_ffn, out_cotangent):
    weight_set = tuple((w.astype(jnp.float32) for w in (w_query, w_key, w_value, w_out, w_gate, w_up, w_down, gain_attn, gain_ffn)))
    position, ancestry, segment, live_slot = jax.vmap(layout)(seg_starts, seg_parents)

    def forward(inputs, weights):

        def tree_step(carry, tree_items):
            return (carry, tree_forward(tree_items[0], weights, tree_items[1], tree_items[2], tree_items[3]))
        return lax.scan(tree_step, jnp.zeros((), jnp.float32), (inputs, position, ancestry, segment))[1]
    outputs, pullback = jax.vjp(forward, layer_in.astype(jnp.float32), weight_set)
    upstream = out_cotangent.astype(jnp.float32) * live_slot.astype(jnp.float32)[..., None]
    input_grad, weight_grads = pullback(upstream)
    return (outputs.astype(jnp.bfloat16), input_grad.astype(jnp.bfloat16), weight_grads[0], weight_grads[1], weight_grads[2], weight_grads[3], weight_grads[4], weight_grads[5], weight_grads[6], weight_grads[7], weight_grads[8])
```

```python
import functools
import jax
import jax.numpy as jnp
from jax import lax
from jax.experimental import pallas as pl
from jax.experimental.pallas import tpu as pltpu
from jax.sharding import PartitionSpec as P

HEAD_DIM = 80
TRUNK = 768
SEGS = 13
TILE = 128
NBRANCH = 4
SEG_TILES = TRUNK // TILE + SEGS - 1
TRUNK_TILES = TRUNK // TILE
LANES = 128
epsilon = 1e-05
masked_score = -1e30
rope_theta = 10000.0
log2e = 1.4426950408889634


def pad_lanes(width):
    return -(-width // LANES) * LANES


def turn_tables():
    half = HEAD_DIM // 2
    frequency = jnp.power(rope_theta, -2.0 * lax.iota(jnp.float32, half) / HEAD_DIM)
    angle = lax.iota(jnp.float32, TRUNK + 2 * TILE)[:, None] * frequency[None, :]
    cosine, sine = jnp.cos(angle), jnp.sin(angle)
    none = jnp.zeros_like(sine)
    tail = jnp.zeros((angle.shape[0], LANES - HEAD_DIM), jnp.float32)
    return jnp.stack(
        [
            jnp.concatenate([cosine, cosine, tail], axis=1),
            jnp.concatenate([none, sine, tail], axis=1),
            jnp.concatenate([-sine, none, tail], axis=1),
        ]
    )


def tile_base(tile):
    return jnp.where(
        tile < TRUNK_TILES,
        tile * TILE,
        jnp.where(tile < TRUNK_TILES + NBRANCH, TRUNK, TRUNK + TILE),
    )


def take_head(rows, head):
    width = rows.shape[1]
    shift = (width - head * HEAD_DIM) % width
    return (pltpu.roll(rows, shift, 1) if shift else rows)[:, :LANES]


def put_head(part, head, width):
    wide = jnp.concatenate(
        [part, jnp.zeros((part.shape[0], width - LANES), part.dtype)], axis=1
    )
    return pltpu.roll(wide, head * HEAD_DIM, 1) if head else wide


def turn(rows, tables, sign):
    half = HEAD_DIM // 2
    cosine, up, down = tables
    swapped = pltpu.roll(rows, half, 1) * up + pltpu.roll(rows, LANES - half, 1) * down
    return rows * cosine + swapped if sign > 0 else rows * cosine - swapped


def head_lanes(rows):
    lane = lax.broadcasted_iota(jnp.int32, rows.shape, 1)
    return jnp.where(lane < HEAD_DIM, rows, 0.0)


def read_rows(ref, start):
    aligned = pl.multiple_of(start // 8 * 8, 8)
    rows = ref[pl.ds(aligned, TILE + 8), :]
    return pltpu.roll(rows, (TILE + 8) - (start - aligned), 0)[:TILE]


def write_rows(ref, start, rows):
    aligned = pl.multiple_of(start // 8 * 8, 8)
    offset = start - aligned
    at = pl.ds(aligned, TILE + 8)
    wide = jnp.concatenate([rows, jnp.zeros((8, rows.shape[1]), rows.dtype)], axis=0)
    wide = pltpu.roll(wide, offset, 0)
    index = lax.broadcasted_iota(jnp.int32, wide.shape, 0)
    inside = (index >= offset) & (index < offset + TILE)
    ref[at, :] = jnp.where(inside, wide, ref[at, :])


def nt(a, b):
    return lax.dot_general(a, b, (((1,), (1,)), ((), ())), preferred_element_type=jnp.float32)


def nn(a, b):
    return lax.dot_general(a, b, (((1,), (0,)), ((), ())), preferred_element_type=jnp.float32)


def causal(columns):
    key = lax.broadcasted_iota(jnp.int32, (TILE, columns), 0)
    query = lax.broadcasted_iota(jnp.int32, (TILE, columns), 1) % TILE
    return key <= query


def each_tile(tile_fn, parent_of):
    for tile in range(TRUNK_TILES):
        tile_fn(tile, tile * TILE, None)

    @pl.loop(TRUNK_TILES, TRUNK_TILES + NBRANCH)
    def _(tile):
        tile_fn(tile, TRUNK, None)

    @pl.loop(TRUNK_TILES + NBRANCH, SEG_TILES)
    def _(tile):
        tile_fn(tile, TRUNK, parent_of(tile) + TRUNK_TILES - 1)


def tile_rows(tile, size=TILE):
    if isinstance(tile, int):
        return pl.ds(tile * size, size)
    return pl.ds(pl.multiple_of(tile * size, size), size)


def forward_kernel(
    group, starts, parents, order, qkv, tables,
    attended, q_keep, k_keep, v_keep, lse_keep,
    slots, v_turned, out_rows,
):
    slot_count = qkv.shape[0] * qkv.shape[1]
    width = slots.shape[1]
    out_width = out_rows.shape[1]
    block = qkv.shape[1]

    @pl.loop(0, qkv.shape[0])
    def _(i):
        slots[pl.ds(pl.multiple_of(order[i] * block, 8), block), :] = qkv[i]

    @pl.loop(0, slot_count // TILE)
    def _(i):
        rows = tile_rows(i)
        own = take_head(slots[rows, :], group + 1)
        own = head_lanes(own).astype(jnp.bfloat16).astype(jnp.float32)
        total = put_head(own, 0, out_width)
        for head in range(1, group):
            total = total + put_head(own, head, out_width)
        out_rows[rows, :] = total

    @pl.loop(0, SEG_TILES)
    def _(tile):
        rows = read_rows(slots, starts[tile])
        base = pl.ds(pl.multiple_of(tile_base(tile), TILE), TILE)
        turns = tuple(tables[t, base, :] for t in range(3))
        for head in range(group):
            turned = turn(take_head(rows, head), turns, 1) * (HEAD_DIM**-0.5 * log2e)
            at = pl.ds(pl.multiple_of(tile * (group * TILE) + head * TILE, TILE), TILE)
            q_keep[at, :] = turned.astype(jnp.bfloat16)
        k_keep[tile_rows(tile), :] = turn(take_head(rows, group), turns, 1).astype(jnp.bfloat16)
        own = head_lanes(take_head(rows, group + 1))
        v_keep[tile_rows(tile), :] = own.astype(jnp.bfloat16)
        v_turned[:, tile_rows(tile)] = own.T.astype(jnp.bfloat16)

    columns = group * TILE

    def attend(tile, full, parent):
        queries = q_keep[tile_rows(tile, columns), :]
        keys = [pl.ds(0, full)] if full else []
        if parent is not None:
            keys.append(tile_rows(parent))
        keys.append(tile_rows(tile))
        scores = [nt(k_keep[at, :], queries) for at in keys]
        scores[-1] = jnp.where(causal(columns), scores[-1], masked_score)
        top = functools.reduce(jnp.maximum, [jnp.max(s, axis=0, keepdims=True) for s in scores])
        weights = [jnp.exp2(s - top) for s in scores]
        total = functools.reduce(jnp.add, [jnp.sum(w, axis=0, keepdims=True) for w in weights])
        mixed = functools.reduce(
            jnp.add,
            [nn(v_turned[:, at], w.astype(jnp.bfloat16)) for at, w in zip(keys, weights)],
        )
        mixed = mixed * (1.0 / total)
        lse_keep[pl.ds(tile, 1)] = (top + jnp.log2(total))[None]
        result = put_head(mixed[:, :TILE].T, 0, out_width)
        for head in range(1, group):
            result = result + put_head(
                mixed[:, head * TILE : (head + 1) * TILE].T, head, out_width
            )
        write_rows(out_rows, starts[tile], result)

    each_tile(attend, lambda tile: parents[tile - TRUNK_TILES + 1])

    kept = attended.shape[-1]

    @pl.loop(0, qkv.shape[0])
    def _(i):
        rows = out_rows[pl.ds(pl.multiple_of(order[i] * block, 8), block), :]
        attended[i] = rows[:, :kept].astype(jnp.bfloat16)


def backward_kernel(
    group, starts, parents, order, attended_grad, q_keep, k_keep, v_keep, lse_keep, tables,
    grads,
    slots, do_keep, k_turned, dk, dv, dq, out_rows,
):
    slot_count = attended_grad.shape[0] * attended_grad.shape[1]
    in_width = slots.shape[1]
    width = out_rows.shape[1]
    block = attended_grad.shape[1]
    kept = attended_grad.shape[2]
    columns = group * TILE

    slots[...] = jnp.zeros_like(slots)

    @pl.loop(0, attended_grad.shape[0])
    def _(i):
        at = pl.ds(pl.multiple_of(order[i] * block, 8), block)
        slots[at, :kept] = attended_grad[i].astype(jnp.float32)

    @pl.loop(0, slot_count // TILE)
    def _(i):
        rows = slots[tile_rows(i), :]
        total = take_head(rows, 0)
        for head in range(1, group):
            total = total + take_head(rows, head)
        out_rows[tile_rows(i), :] = put_head(head_lanes(total), group + 1, width)

    @pl.loop(0, SEG_TILES)
    def _(tile):
        rows = read_rows(slots, starts[tile])
        for head in range(group):
            at = pl.ds(pl.multiple_of(tile * columns + head * TILE, TILE), TILE)
            do_keep[at, :] = head_lanes(take_head(rows, head)).astype(jnp.bfloat16)
        k_turned[:, tile_rows(tile)] = (
            k_keep[tile_rows(tile), :].astype(jnp.float32).T.astype(jnp.bfloat16)
        )

    dk[...] = jnp.zeros_like(dk)
    dv[...] = jnp.zeros_like(dv)

    def attend(tile, full, parent):
        queries = q_keep[tile_rows(tile, columns), :]
        upward = do_keep[tile_rows(tile, columns), :]
        lse = lse_keep[pl.ds(tile, 1)][0]
        keys = [pl.ds(0, full)] if full else []
        if parent is not None:
            keys.append(tile_rows(parent))
        keys.append(tile_rows(tile))
        probs = [jnp.exp2(nt(k_keep[at, :], queries) - lse) for at in keys]
        probs[-1] = jnp.where(causal(columns), probs[-1], 0.0)
        prob_grads = [nt(v_keep[at, :], upward) for at in keys]
        row_dot = functools.reduce(
            jnp.add,
            [jnp.sum(p * g, axis=0, keepdims=True) for p, g in zip(probs, prob_grads)],
        )
        mixed = None
        for at, p, g in zip(keys, probs, prob_grads):
            score_grad = (p * (g - row_dot)).astype(jnp.bfloat16)
            dv[at, :] += nn(p.astype(jnp.bfloat16), upward)
            dk[at, :] += nn(score_grad, queries)
            part = nn(k_turned[:, at], score_grad)
            mixed = part if mixed is None else mixed + part
        base = pl.ds(pl.multiple_of(tile_base(tile), TILE), TILE)
        turns = tuple(tables[t, base, :] for t in range(3))
        result = None
        for head in range(group):
            part = turn(mixed[:, head * TILE : (head + 1) * TILE].T, turns, -1) * HEAD_DIM**-0.5
            part = put_head(part, head, width)
            result = part if result is None else result + part
        dq[tile_rows(tile), :] = result

    each_tile(attend, lambda tile: parents[tile - TRUNK_TILES + 1])

    @pl.loop(0, SEG_TILES)
    def _(tile):
        rows = tile_rows(tile)
        base = pl.ds(pl.multiple_of(tile_base(tile), TILE), TILE)
        turns = tuple(tables[t, base, :] for t in range(3))
        key_part = turn(dk[rows, :], turns, -1) * (1.0 / log2e)
        total = dq[rows, :] + put_head(key_part, group, width)
        total = total + put_head(dv[rows, :], group + 1, width)
        write_rows(out_rows, starts[tile], total)

    @pl.loop(0, attended_grad.shape[0])
    def _(i):
        rows = out_rows[pl.ds(pl.multiple_of(order[i] * block, 8), block), :]
        grads[i] = rows[:, : grads.shape[2]].astype(jnp.bfloat16)


SMEM = pl.BlockSpec(memory_space=pltpu.SMEM)
VMEM = pl.BlockSpec(memory_space=pltpu.VMEM)


def attend_forward(group, qkv, tables, starts, parents, order):
    blocks, block, width = qkv.shape
    slot_count = blocks * block
    wide = pad_lanes(width)
    out_wide = pad_lanes(group * HEAD_DIM)
    live = SEG_TILES * TILE
    return pl.pallas_call(
        functools.partial(forward_kernel, group),
        out_shape=(
            jax.ShapeDtypeStruct((blocks, block, group * HEAD_DIM), jnp.bfloat16),
            jax.ShapeDtypeStruct((group * live, LANES), jnp.bfloat16),
            jax.ShapeDtypeStruct((live, LANES), jnp.bfloat16),
            jax.ShapeDtypeStruct((live, LANES), jnp.bfloat16),
            jax.ShapeDtypeStruct((SEG_TILES, 1, group * TILE), jnp.float32),
        ),
        in_specs=[SMEM, SMEM, SMEM, VMEM, VMEM],
        out_specs=(VMEM,) * 5,
        scratch_shapes=[
            pltpu.VMEM((slot_count + 8, wide), jnp.float32),
            pltpu.VMEM((LANES, live), jnp.bfloat16),
            pltpu.VMEM((slot_count + 8, out_wide), jnp.float32),
        ],
        compiler_params=pltpu.CompilerParams(vmem_limit_bytes=48 * 2**20),
        name="tree_forward",
    )(starts, parents, order, qkv, tables)


def attend_backward(attended_grad, kept, tables, starts, parents, order):
    blocks, block, width = attended_grad.shape
    slot_count = blocks * block
    group = width // HEAD_DIM
    wide = pad_lanes((group + 2) * HEAD_DIM + 2)
    in_wide = pad_lanes(width)
    live = SEG_TILES * TILE
    return pl.pallas_call(
        functools.partial(backward_kernel, group),
        out_shape=jax.ShapeDtypeStruct((blocks, block, wide), jnp.bfloat16),
        in_specs=[SMEM, SMEM, SMEM] + [VMEM] * 6,
        out_specs=VMEM,
        scratch_shapes=[
            pltpu.VMEM((slot_count + 8, in_wide), jnp.float32),
            pltpu.VMEM((group * live, LANES), jnp.bfloat16),
            pltpu.VMEM((LANES, live), jnp.bfloat16),
            pltpu.VMEM((live, LANES), jnp.float32),
            pltpu.VMEM((live, LANES), jnp.float32),
            pltpu.VMEM((live, wide), jnp.float32),
            pltpu.VMEM((slot_count + 8, wide), jnp.float32),
        ],
        compiler_params=pltpu.CompilerParams(vmem_limit_bytes=56 * 2**20),
        name="tree_backward",
    )(starts, parents, order, attended_grad, *kept, tables)


def window(ref, rows, start, size, wide, at):
    full = ref.shape[-1]
    span = min(pad_lanes(size + LANES - 1), full)
    aligned = jnp.minimum(start // LANES * LANES, full - span)
    shift = start - aligned
    values = ref[rows, pl.ds(pl.multiple_of(aligned, LANES), span)].astype(jnp.float32)
    lane = lax.broadcasted_iota(jnp.int32, values.shape, 1)
    values = jnp.where((lane >= shift) & (lane < shift + size), values, 0.0)
    reach = max(span, wide)
    if reach > span:
        filling = jnp.zeros((values.shape[0], reach - span), values.dtype)
        values = jnp.concatenate([values, filling], axis=1)
    return pltpu.roll(values, lax.rem(at - shift + reach, reach), 1)[:, :wide]


def pack_kernel(places, extras, step, me, *refs):
    sources, gains = refs[: len(places)], refs[len(places) : len(places) + extras]
    blocks = refs[len(places) + extras :]
    count = len(blocks)
    wide = blocks[0].shape[1]
    extra_at = sum(size for size, _ in places)

    @pl.loop(0, blocks[0].shape[0] // step)
    def _(i):
        rows = pl.ds(pl.multiple_of(i * step, step), step)
        lane = lax.broadcasted_iota(jnp.int32, (step, wide), 1)
        for way in range(count):
            total = None
            for ref, (size, at) in zip(sources, places):
                part = window(ref, rows, (me[0] ^ way) * size, size, wide, at)
                total = part if total is None else total + part
            for index, gain in enumerate(gains):
                total = jnp.where(lane == extra_at + index, gain[rows, :].astype(jnp.float32), total)
            blocks[way][rows, :] = total.astype(jnp.bfloat16)


def pack(weights, gains, me, places, wide, count):
    rows = weights[0].shape[0]
    return pl.pallas_call(
        functools.partial(pack_kernel, places, len(gains), 16),
        out_shape=(jax.ShapeDtypeStruct((rows, wide), jnp.bfloat16),) * count,
        in_specs=[SMEM] + [VMEM] * (len(weights) + len(gains)),
        out_specs=(VMEM,) * count,
        compiler_params=pltpu.CompilerParams(vmem_limit_bytes=48 * 2**20),
        name="pack_weights",
    )(me[None], *weights, *[gain[:, None] for gain in gains])


def assemble_kernel(count, extra_at, me, *refs):
    blocks, whole = refs[:count], refs[count]
    rows = blocks[0].shape[0]
    for way, block in enumerate(blocks):
        at = pl.ds(pl.multiple_of((me[0] ^ way) * rows, 16), rows)
        whole[at, :] = block[...]
    if extra_at is not None:
        gains = refs[count + 1]
        first = extra_at // LANES * LANES
        for index in range(whole.shape[0] // LANES):
            at = pl.ds(index * LANES, LANES)
            part = whole[at, first : first + LANES].astype(jnp.float32).T
            gains[:, at] = pltpu.roll(part, LANES - extra_at % LANES, 0)[:8]


def assemble(blocks, me, extra_at):
    rows, wide = blocks[0].shape
    shape = (len(blocks) * rows, wide)
    out_shape = (jax.ShapeDtypeStruct(shape, jnp.bfloat16),)
    if extra_at is not None:
        out_shape += (jax.ShapeDtypeStruct((8, shape[0]), jnp.float32),)
    return pl.pallas_call(
        functools.partial(assemble_kernel, len(blocks), extra_at),
        out_shape=out_shape,
        in_specs=[SMEM] + [VMEM] * len(blocks),
        out_specs=(VMEM,) * len(out_shape),
        compiler_params=pltpu.CompilerParams(vmem_limit_bytes=48 * 2**20),
        name="assemble_weights",
    )(me[None], *blocks)


def after(values, *earlier):
    anywhere = pl.BlockSpec(memory_space=pl.ANY)
    return pl.pallas_call(
        lambda *refs: None,
        out_shape=tuple(jax.ShapeDtypeStruct(v.shape, v.dtype) for v in values),
        in_specs=[anywhere] * (len(values) + len(earlier)),
        out_specs=(anywhere,) * len(values),
        input_output_aliases={i: i for i in range(len(values))},
        name="after",
    )(*values, *earlier)


def spread_kernel(places, count, me, *refs):
    blocks = refs[:count]
    weights = refs[count : count + len(places)]
    outs = refs[count + len(places) : count + 2 * len(places)]
    gain, held = refs[count + 2 * len(places) :]
    for way in range(count):
        held[me[0] ^ way] = blocks[way][...].astype(jnp.float32)
    for out in outs:
        out[...] = jnp.zeros_like(out)
    total = jnp.zeros(gain.shape, jnp.float32)
    for (size, at), weight, out in zip(places, weights, outs):
        full = out.shape[1]
        for index in range(count):
            start = index * size
            span = min(pad_lanes(size + start % LANES), full)
            aligned = min(start // LANES * LANES, full - span)
            shift = start - aligned
            low_lane = at // LANES * LANES
            width = pad_lanes(at - low_lane + size)
            values = held[index][:, low_lane : low_lane + width]
            lane = lax.broadcasted_iota(jnp.int32, values.shape, 1)
            inside = (lane >= at - low_lane) & (lane < at - low_lane + size)
            values = jnp.where(inside, values, 0.0)
            reach = max(span, width)
            if reach > width:
                filling = jnp.zeros((values.shape[0], reach - width), values.dtype)
                values = jnp.concatenate([values, filling], axis=1)
            turned = (shift - (at - low_lane)) % reach
            values = (pltpu.roll(values, turned, 1) if turned else values)[:, :span]
            out[:, aligned : aligned + span] += values
        product = out[...] * weight[...].astype(jnp.float32)
        total = total + jnp.sum(product, axis=1, keepdims=True)
    gain[...] = total


def spread(blocks, weights, me, places, step):
    count = len(blocks)
    rows, wide = blocks[0].shape
    tile = lambda width: pl.BlockSpec((step, width), lambda i: (i, 0))
    return pl.pallas_call(
        functools.partial(spread_kernel, places, count),
        grid=(rows // step,),
        out_shape=tuple(jax.ShapeDtypeStruct(w.shape, jnp.float32) for w in weights)
        + (jax.ShapeDtypeStruct((rows, 1), jnp.float32),),
        in_specs=[SMEM] + [tile(wide)] * count + [tile(w.shape[1]) for w in weights],
        out_specs=tuple(tile(w.shape[1]) for w in weights) + (tile(1),),
        scratch_shapes=[pltpu.VMEM((count, step, wide), jnp.float32)],
        compiler_params=pltpu.CompilerParams(vmem_limit_bytes=56 * 2**20),
        name="spread_gradients",
    )(me[None], *blocks, *weights)


def normed(values):
    inverse = lax.rsqrt(jnp.mean(values * values, axis=-1, keepdims=True) + epsilon)
    return (values * inverse, inverse)


def norm_back(upward, unit_rows, inverse):
    return inverse * (upward - unit_rows * jnp.mean(upward * unit_rows, axis=-1, keepdims=True))


def layout(starts, slot_count):
    slot_index = lax.iota(jnp.int32, slot_count)
    segment_ids = lax.iota(jnp.int32, SEGS)
    segment_len = jnp.where(segment_ids == 0, TRUNK, TILE)
    inside = (slot_index[None, :] >= starts[:, None]) & (
        slot_index[None, :] < (starts + segment_len)[:, None]
    )
    return jnp.any(inside, axis=0)


def dot(left, right):
    return jnp.dot(left, right, preferred_element_type=jnp.float32)


def transpose_dot(left, right):
    return lax.dot_general(
        left, right, (((1,), (1,)), ((), ())), preferred_element_type=jnp.float32
    )


def rows_dot(left, right):
    return lax.dot_general(
        left, right, (((0,), (0,)), ((), ())), preferred_element_type=jnp.float32
    )


def low(values):
    return values.astype(jnp.bfloat16)


def plain(count):
    return count != 8


def gather_order(count):
    if plain(count):
        return [list(range(count))] * count
    ways = ((0, 1, 2, 3, 5, 4, 6, 7), (0, 1, 4, 5, 3, 2, 6, 7))
    return [[index ^ way for way in ways[index % 2]] for index in range(count)]


def swap_core(values):
    return lax.ppermute(values, "slot", [(i, i ^ 1) for i in range(8)])


def swap_near(values):
    return lax.ppermute(values, "slot", [(i, i ^ (4 if i % 2 else 2)) for i in range(8)])


def swap_far(values):
    return lax.ppermute(values, "slot", [(i, i ^ (2 if i % 2 else 4)) for i in range(8)])


def gather(own):
    count = lax.axis_size("slot")
    if plain(count):
        return [lax.all_gather(own, "slot", axis=0, tiled=True)]
    block = own.shape[0]
    chip = jnp.concatenate([own, swap_core(own)], axis=0)
    near = swap_near(chip)
    corner = swap_far(near[:block])
    return [chip, near, swap_core(near), jnp.concatenate([corner, swap_core(corner)], axis=0)]


def scatter(parts):
    count = lax.axis_size("slot")
    if plain(count):
        return lax.psum_scatter(parts[0], "slot", scatter_dimension=0, tiled=True).astype(
            jnp.float32
        )
    chip, near, side, corner = parts
    block = chip.shape[0] // 2
    wide = lambda values: values.astype(jnp.float32)
    near_sum = low(wide(near) + wide(swap_core(side)))
    other = low(wide(chip[block:]) + wide(swap_near(near_sum[block:])))
    corner_sum = low(wide(corner[:block]) + wide(swap_core(corner[block:])))
    near_own = low(wide(near_sum[:block]) + wide(swap_far(corner_sum)))
    return wide(chip[:block]) + wide(swap_near(near_own)) + wide(swap_core(other))


def send(block, way):
    count = lax.axis_size("slot")
    if way == 0:
        return block
    return lax.ppermute(block, "slot", [(i, i ^ way) for i in range(count)])


def sum_trees(part):
    count = lax.axis_size("replica")
    if count != 4:
        return lax.psum(part, "replica")
    place = lax.axis_index("replica")
    wide = lambda values: values.astype(jnp.float32)
    pair = low(wide(part) + wide(lax.ppermute(part, "replica", [(0, 1), (3, 2)])))
    total = low(wide(pair) + wide(lax.ppermute(pair, "replica", [(1, 2), (2, 1)])))
    back = lax.ppermute(total, "replica", [(1, 0), (2, 3)])
    return jnp.where((place == 0) | (place == 3), back, total)


def to_columns(weights, gains, places, wide, heads_in, earlier=()):
    count = lax.axis_size("slot")
    me = lax.axis_index("slot")
    extra_at = sum(size for size, _ in places) if gains else None
    if plain(count):
        blocks = jnp.zeros((count, weights[0].shape[0], wide), jnp.bfloat16)
        for weight, (size, at), heads in zip(weights, places, heads_in):
            blocks = blocks.at[:, :, at : at + size].set(split_columns(weight, count, heads))
        for index, gain in enumerate(gains):
            blocks = blocks.at[:, :, extra_at + index].set(gain[None])
        whole = lax.all_to_all(blocks, "slot", 0, 0).reshape(-1, wide)
        if not gains:
            return (whole,)
        return whole, whole[:, extra_at : extra_at + len(gains)].T.astype(jnp.float32)
    blocks = pack(weights, gains, me, places, wide, count)
    if earlier:
        blocks = after(blocks, *earlier)
    return assemble([send(block, way) for way, block in enumerate(blocks)], me, extra_at)


def to_rows(gradient, weights, places, heads_in, group, step):
    count = lax.axis_size("slot")
    me = lax.axis_index("slot")
    rows = gradient.shape[0] // count
    if plain(count):
        blocks = lax.all_to_all(gradient.reshape(count, rows, -1), "slot", 0, 0)
        blocks = sum_trees(blocks).astype(jnp.float32)
        parts = [
            join_columns(blocks[:, :, at : at + size], heads)
            for (size, at), heads in zip(places, heads_in)
        ]
        products = [jnp.sum(p * w.astype(jnp.float32), axis=1) for p, w in zip(parts, weights)]
        return parts, sum(products)
    arrived = [None] * count
    for base in reversed(range(0, count, group)):
        first = (me ^ base) // group * group * rows
        summed = sum_trees(lax.dynamic_slice_in_dim(gradient, first, group * rows))
        for way in range(base, base + group):
            block = summed
            if group > 1:
                block = lax.dynamic_slice_in_dim(summed, (me ^ way) % group * rows, rows)
            arrived[way] = send(block, way)
    *parts, product = spread(arrived, weights, me, places, step)
    return parts, product[:, 0]


def split_columns(weight, count, heads_in=None):
    rows, columns = weight.shape
    if heads_in is not None and heads_in < count:
        weight = weight.reshape(rows, heads_in, columns // heads_in)
        weight = jnp.repeat(weight, count // heads_in, axis=1)
    else:
        weight = weight.reshape(rows, count, columns // count)
    return weight.transpose(1, 0, 2)


def join_columns(blocks, heads_in=None):
    count, rows, columns = blocks.shape
    if heads_in is not None and heads_in < count:
        blocks = jnp.sum(blocks.reshape(heads_in, count // heads_in, rows, columns), axis=1)
        count = heads_in
    return blocks.transpose(1, 0, 2).reshape(rows, count * columns)


def shards(
    layer_in,
    seg_starts,
    seg_parents,
    w_query,
    w_key,
    w_value,
    w_out,
    w_gate,
    w_up,
    w_down,
    gain_attn,
    gain_ffn,
    out_cotangent,
):
    count = lax.axis_size("slot")
    me = lax.axis_index("slot")
    row_count = layer_in.shape[1]
    slot_count = row_count * count
    features = layer_in.shape[2]
    kv_heads = w_key.shape[1] // HEAD_DIM
    q_width = w_query.shape[1] // count
    heads_width = q_width + 2 * HEAD_DIM
    heads_wide = pad_lanes(heads_width + 2)
    hidden = w_down.shape[0]
    hidden_wide = pad_lanes(hidden)
    starts, parents = seg_starts[0], seg_parents[0]
    tile_starts = jnp.concatenate([lax.iota(jnp.int32, TRUNK_TILES) * TILE, starts[1:]])
    order = jnp.asarray(gather_order(count), jnp.int32)[me]
    tables = turn_tables()
    live = layout(starts, slot_count).astype(jnp.float32).reshape(count, row_count)
    my_live = live[me]
    live = live[order].reshape(slot_count)

    def cut(values):
        return jnp.split(values, 1 if plain(count) else 4, axis=0)

    def blocks_of(parts):
        return jnp.concatenate(parts, axis=0).reshape(count, row_count, parts[0].shape[-1])

    layer_parts = gather(layer_in[0])
    head_weights = (w_query, w_key, w_value)
    head_places = ((q_width, 0), (HEAD_DIM, q_width), (HEAD_DIM, q_width + HEAD_DIM))
    head_counts = (None, kv_heads, kv_heads)
    w_heads, gains = to_columns(
        head_weights, (gain_attn, gain_ffn), head_places, heads_wide, head_counts
    )
    full_gain_attn, full_gain_ffn = gains[0], gains[1]
    attn_parts = [
        low(normed(part.astype(jnp.float32))[0] * full_gain_attn) for part in layer_parts
    ]
    qkv = blocks_of([dot(part, w_heads) for part in attn_parts])
    attended, *kept = attend_forward(q_width // HEAD_DIM, qkv, tables, tile_starts, parents, order)
    attended = attended.reshape(slot_count, q_width)
    residual = layer_in[0].astype(jnp.float32)
    middle = residual + scatter([low(dot(part, w_out)) for part in cut(attended)])

    hidden_places = ((hidden, 0), (hidden, hidden_wide))
    (w_hidden,) = to_columns(
        (w_gate, w_up), (), hidden_places, 2 * hidden_wide, (None, None), (w_heads, layer_parts[-1])
    )
    w_lower = jnp.pad(w_down, ((0, hidden_wide - hidden), (0, 0)))
    unit_ffn, rms_ffn = normed(middle)
    ffn_parts = gather(low(unit_ffn * full_gain_ffn))
    late_cotangent = out_cotangent[0]
    if not plain(count):
        (late_cotangent,) = after((late_cotangent,), w_hidden)
    down_parts = [
        low(part.astype(jnp.float32) * mask[:, None])
        for part, mask in zip(gather(late_cotangent), cut(live))
    ]
    active_parts, hidden_grads = [], []
    for ffn_part, down_part in zip(ffn_parts, down_parts):
        both = dot(ffn_part, w_hidden)
        gate, up = both[:, :hidden_wide], both[:, hidden_wide:]
        sigmoid = jax.nn.sigmoid(gate)
        silu = gate * sigmoid
        active_parts.append(low(silu * up))
        active_grad = transpose_dot(down_part, w_lower)
        gate_grad = low(active_grad * up * sigmoid * (1.0 + gate * (1.0 - sigmoid)))
        hidden_grads.append(jnp.concatenate([gate_grad, low(active_grad * silu)], axis=1))
    ffn_input_grad = scatter([low(transpose_dot(part, w_hidden)) for part in hidden_grads])
    layer_out = low(middle + scatter([low(dot(part, w_lower)) for part in active_parts]))
    grad_down = rows_dot(
        jnp.concatenate(active_parts, axis=0), jnp.concatenate(down_parts, axis=0)
    )[:hidden]
    grad_hidden = low(
        rows_dot(jnp.concatenate(ffn_parts, axis=0), jnp.concatenate(hidden_grads, axis=0))
    )
    upstream = out_cotangent[0].astype(jnp.float32) * my_live[:, None]
    middle_grad = upstream + norm_back(ffn_input_grad * full_gain_ffn, unit_ffn, rms_ffn)

    branch_parts = gather(low(middle_grad))
    attended_grad = blocks_of([low(transpose_dot(part, w_out)) for part in branch_parts])
    head_grads = attend_backward(attended_grad, kept, tables, tile_starts, parents, order)
    head_parts = cut(head_grads.reshape(slot_count, heads_wide))
    attn_input_grad = scatter(
        [low(transpose_dot(part, w_heads)) for part in head_parts]
    )
    grad_proj = sum(rows_dot(a, b) for a, b in zip(cut(attended), branch_parts))
    grad_heads = low(sum(rows_dot(a, b) for a, b in zip(attn_parts, head_parts)))
    unit_attn, rms_attn = normed(residual)
    grad_in = low(
        middle_grad + norm_back(attn_input_grad * full_gain_attn, unit_attn, rms_attn)
    )

    grad_down = sum_trees(low(grad_down)).astype(jnp.float32)
    (grad_gate, grad_up), gain_ffn_sum = to_rows(
        grad_hidden, (w_gate, w_up), hidden_places, (None, None), 2, 32
    )
    grad_proj = sum_trees(low(grad_proj)).astype(jnp.float32)
    (grad_query, grad_key, grad_value), gain_attn_sum = to_rows(
        grad_heads, head_weights, head_places, head_counts, 4, 64
    )
    return (
        layer_out[None],
        grad_in[None],
        grad_query,
        grad_key,
        grad_value,
        grad_proj,
        grad_gate,
        grad_up,
        grad_down,
        gain_attn_sum / gain_attn.astype(jnp.float32),
        gain_ffn_sum / gain_ffn.astype(jnp.float32),
    )


def solution(mesh):
    tokens, tree, rows, vector = P("replica", "slot", None), P("replica", None), P("slot", None), P("slot")
    in_specs = (tokens, tree, tree) + (rows,) * 7 + (vector, vector, tokens)
    out_specs = (tokens, tokens) + (rows,) * 7 + (vector, vector)
    return jax.shard_map(shards, mesh=mesh, in_specs=in_specs, out_specs=out_specs, check_vma=False)
```

```python
import functools
import jax
import jax.numpy as jnp
from jax import lax
from jax.experimental import pallas as pl
from jax.experimental.pallas import tpu as pltpu
from jax.sharding import PartitionSpec as P

HEAD_DIM = 80
TRUNK = 768
SEGS = 13
TILE = 128
NBRANCH = 4
SEG_TILES = TRUNK // TILE + SEGS - 1
TRUNK_TILES = TRUNK // TILE
LANES = 128
BLOCK = 256
epsilon = 1e-05
masked_score = -1e30
rope_theta = 10000.0
log2e = 1.4426950408889634


def pad_lanes(width):
    return -(-width // LANES) * LANES


def turn_tables():
    half = HEAD_DIM // 2
    frequency = jnp.power(rope_theta, -2.0 * lax.iota(jnp.float32, half) / HEAD_DIM)
    angle = lax.iota(jnp.float32, TRUNK + 2 * TILE)[:, None] * frequency[None, :]
    cosine, sine = jnp.cos(angle), jnp.sin(angle)
    none = jnp.zeros_like(sine)
    tail = jnp.zeros((angle.shape[0], LANES - HEAD_DIM), jnp.float32)
    return jnp.stack(
        [
            jnp.concatenate([cosine, cosine, tail], axis=1),
            jnp.concatenate([none, sine, tail], axis=1),
            jnp.concatenate([-sine, none, tail], axis=1),
        ]
    )


def tile_base(tile):
    return jnp.where(
        tile < TRUNK_TILES,
        tile * TILE,
        jnp.where(tile < TRUNK_TILES + NBRANCH, TRUNK, TRUNK + TILE),
    )


def take_head(rows, head):
    width = rows.shape[1]
    shift = (width - head * HEAD_DIM) % width
    return (pltpu.roll(rows, shift, 1) if shift else rows)[:, :LANES]


def put_head(part, head, width):
    wide = jnp.concatenate(
        [part, jnp.zeros((part.shape[0], width - LANES), part.dtype)], axis=1
    )
    return pltpu.roll(wide, head * HEAD_DIM, 1) if head else wide


def turn(rows, tables, sign):
    half = HEAD_DIM // 2
    cosine, up, down = tables
    swapped = pltpu.roll(rows, half, 1) * up + pltpu.roll(rows, LANES - half, 1) * down
    return rows * cosine + swapped if sign > 0 else rows * cosine - swapped


def head_lanes(rows):
    lane = lax.broadcasted_iota(jnp.int32, rows.shape, 1)
    return jnp.where(lane < HEAD_DIM, rows, 0.0)


def read_rows(ref, start):
    aligned = pl.multiple_of(start // 8 * 8, 8)
    rows = ref[pl.ds(aligned, TILE + 8), :]
    return pltpu.roll(rows, (TILE + 8) - (start - aligned), 0)[:TILE]


def write_rows(ref, start, rows):
    aligned = pl.multiple_of(start // 8 * 8, 8)
    offset = start - aligned
    at = pl.ds(aligned, TILE + 8)
    wide = jnp.concatenate([rows, jnp.zeros((8, rows.shape[1]), rows.dtype)], axis=0)
    wide = pltpu.roll(wide, offset, 0)
    index = lax.broadcasted_iota(jnp.int32, wide.shape, 0)
    inside = (index >= offset) & (index < offset + TILE)
    ref[at, :] = jnp.where(inside, wide, ref[at, :])


def nt(a, b):
    return lax.dot_general(a, b, (((1,), (1,)), ((), ())), preferred_element_type=jnp.float32)


def nn(a, b):
    return lax.dot_general(a, b, (((1,), (0,)), ((), ())), preferred_element_type=jnp.float32)


def causal(columns):
    key = lax.broadcasted_iota(jnp.int32, (TILE, columns), 0)
    query = lax.broadcasted_iota(jnp.int32, (TILE, columns), 1) % TILE
    return key <= query


def each_tile(tile_fn, parent_of):
    for tile in range(TRUNK_TILES):
        tile_fn(tile, tile * TILE, None)

    @pl.loop(TRUNK_TILES, TRUNK_TILES + NBRANCH)
    def _(tile):
        tile_fn(tile, TRUNK, None)

    @pl.loop(TRUNK_TILES + NBRANCH, SEG_TILES)
    def _(tile):
        tile_fn(tile, TRUNK, parent_of(tile) + TRUNK_TILES - 1)


def tile_rows(tile, size=TILE):
    if isinstance(tile, int):
        return pl.ds(tile * size, size)
    return pl.ds(pl.multiple_of(tile * size, size), size)


def forward_kernel(
    group, starts, parents, order, qkv, tables,
    attended, q_keep, k_keep, v_keep, lse_keep,
    slots, v_turned, out_rows,
):
    slot_count = qkv.shape[0] * qkv.shape[1]
    width = slots.shape[1]
    out_width = out_rows.shape[1]
    block = qkv.shape[1]

    @pl.loop(0, qkv.shape[0])
    def _(i):
        slots[pl.ds(pl.multiple_of(order[i] * block, 8), block), :] = qkv[i]

    @pl.loop(0, slot_count // TILE)
    def _(i):
        rows = tile_rows(i)
        own = take_head(slots[rows, :], group + 1)
        own = head_lanes(own).astype(jnp.bfloat16).astype(jnp.float32)
        total = put_head(own, 0, out_width)
        for head in range(1, group):
            total = total + put_head(own, head, out_width)
        out_rows[rows, :] = total

    @pl.loop(0, SEG_TILES)
    def _(tile):
        rows = read_rows(slots, starts[tile])
        base = pl.ds(pl.multiple_of(tile_base(tile), TILE), TILE)
        turns = tuple(tables[t, base, :] for t in range(3))
        for head in range(group):
            turned = turn(take_head(rows, head), turns, 1) * (HEAD_DIM**-0.5 * log2e)
            at = pl.ds(pl.multiple_of(tile * (group * TILE) + head * TILE, TILE), TILE)
            q_keep[at, :] = turned.astype(jnp.bfloat16)
        k_keep[tile_rows(tile), :] = turn(take_head(rows, group), turns, 1).astype(jnp.bfloat16)
        own = head_lanes(take_head(rows, group + 1))
        v_keep[tile_rows(tile), :] = own.astype(jnp.bfloat16)
        v_turned[:, tile_rows(tile)] = own.T.astype(jnp.bfloat16)

    columns = group * TILE

    def attend(tile, full, parent):
        queries = q_keep[tile_rows(tile, columns), :]
        keys = [pl.ds(0, full)] if full else []
        if parent is not None:
            keys.append(tile_rows(parent))
        keys.append(tile_rows(tile))
        scores = [nt(k_keep[at, :], queries) for at in keys]
        scores[-1] = jnp.where(causal(columns), scores[-1], masked_score)
        top = functools.reduce(jnp.maximum, [jnp.max(s, axis=0, keepdims=True) for s in scores])
        weights = [jnp.exp2(s - top) for s in scores]
        total = functools.reduce(jnp.add, [jnp.sum(w, axis=0, keepdims=True) for w in weights])
        mixed = functools.reduce(
            jnp.add,
            [nn(v_turned[:, at], w.astype(jnp.bfloat16)) for at, w in zip(keys, weights)],
        )
        mixed = mixed * (1.0 / total)
        lse_keep[pl.ds(tile, 1)] = (top + jnp.log2(total))[None]
        result = put_head(mixed[:, :TILE].T, 0, out_width)
        for head in range(1, group):
            result = result + put_head(
                mixed[:, head * TILE : (head + 1) * TILE].T, head, out_width
            )
        write_rows(out_rows, starts[tile], result)

    each_tile(attend, lambda tile: parents[tile - TRUNK_TILES + 1])

    kept = attended.shape[-1]

    @pl.loop(0, qkv.shape[0])
    def _(i):
        rows = out_rows[pl.ds(pl.multiple_of(order[i] * block, 8), block), :]
        attended[i] = rows[:, :kept].astype(jnp.bfloat16)


def backward_kernel(
    group, starts, parents, order, attended_grad, q_keep, k_keep, v_keep, lse_keep, tables,
    grads,
    slots, do_keep, k_turned, dk, dv, dq, out_rows,
):
    slot_count = attended_grad.shape[0] * attended_grad.shape[1]
    in_width = slots.shape[1]
    width = out_rows.shape[1]
    block = attended_grad.shape[1]
    kept = attended_grad.shape[2]
    columns = group * TILE

    slots[...] = jnp.zeros_like(slots)

    @pl.loop(0, attended_grad.shape[0])
    def _(i):
        at = pl.ds(pl.multiple_of(order[i] * block, 8), block)
        slots[at, :kept] = attended_grad[i].astype(jnp.float32)

    @pl.loop(0, slot_count // TILE)
    def _(i):
        rows = slots[tile_rows(i), :]
        total = take_head(rows, 0)
        for head in range(1, group):
            total = total + take_head(rows, head)
        out_rows[tile_rows(i), :] = put_head(head_lanes(total), group + 1, width)

    @pl.loop(0, SEG_TILES)
    def _(tile):
        rows = read_rows(slots, starts[tile])
        for head in range(group):
            at = pl.ds(pl.multiple_of(tile * columns + head * TILE, TILE), TILE)
            do_keep[at, :] = head_lanes(take_head(rows, head)).astype(jnp.bfloat16)
        k_turned[:, tile_rows(tile)] = (
            k_keep[tile_rows(tile), :].astype(jnp.float32).T.astype(jnp.bfloat16)
        )

    dk[...] = jnp.zeros_like(dk)
    dv[...] = jnp.zeros_like(dv)

    def attend(tile, full, parent):
        queries = q_keep[tile_rows(tile, columns), :]
        upward = do_keep[tile_rows(tile, columns), :]
        lse = lse_keep[pl.ds(tile, 1)][0]
        keys = [pl.ds(0, full)] if full else []
        if parent is not None:
            keys.append(tile_rows(parent))
        keys.append(tile_rows(tile))
        probs = [jnp.exp2(nt(k_keep[at, :], queries) - lse) for at in keys]
        probs[-1] = jnp.where(causal(columns), probs[-1], 0.0)
        prob_grads = [nt(v_keep[at, :], upward) for at in keys]
        row_dot = functools.reduce(
            jnp.add,
            [jnp.sum(p * g, axis=0, keepdims=True) for p, g in zip(probs, prob_grads)],
        )
        mixed = None
        for at, p, g in zip(keys, probs, prob_grads):
            score_grad = (p * (g - row_dot)).astype(jnp.bfloat16)
            dv[at, :] += nn(p.astype(jnp.bfloat16), upward)
            dk[at, :] += nn(score_grad, queries)
            part = nn(k_turned[:, at], score_grad)
            mixed = part if mixed is None else mixed + part
        base = pl.ds(pl.multiple_of(tile_base(tile), TILE), TILE)
        turns = tuple(tables[t, base, :] for t in range(3))
        result = None
        for head in range(group):
            part = turn(mixed[:, head * TILE : (head + 1) * TILE].T, turns, -1) * HEAD_DIM**-0.5
            part = put_head(part, head, width)
            result = part if result is None else result + part
        dq[tile_rows(tile), :] = result

    each_tile(attend, lambda tile: parents[tile - TRUNK_TILES + 1])

    @pl.loop(0, SEG_TILES)
    def _(tile):
        rows = tile_rows(tile)
        base = pl.ds(pl.multiple_of(tile_base(tile), TILE), TILE)
        turns = tuple(tables[t, base, :] for t in range(3))
        key_part = turn(dk[rows, :], turns, -1) * (1.0 / log2e)
        total = dq[rows, :] + put_head(key_part, group, width)
        total = total + put_head(dv[rows, :], group + 1, width)
        write_rows(out_rows, starts[tile], total)

    @pl.loop(0, attended_grad.shape[0])
    def _(i):
        rows = out_rows[pl.ds(pl.multiple_of(order[i] * block, 8), block), :]
        grads[i] = rows[:, : grads.shape[2]].astype(jnp.bfloat16)


def dense_kernel(
    chunk, held, order, x_far, down_far, live_far, w_far, lower_far, *refs
):
    refs = refs[held:]
    whole, out_far, back_far, refs = refs[:4], refs[4], refs[5], refs[6:]
    x, down, live, w, lower, both, upward, active, masked, hidden, back, out, sems = refs
    wide = lower.shape[0]
    blocks = order.shape[0] // 4
    block = x.shape[0] // blocks
    inside = [pl.ds(i * block, block) for i in range(blocks)]
    rows = [
        pl.ds(pl.multiple_of(order[chunk * blocks + i] * block, 16), block) for i in range(blocks)
    ]

    def copies(near, far, first, inward):
        ends = [(near.at[a], far.at[b]) for a, b in zip(inside, rows)]
        return [
            pltpu.make_async_copy(*(reversed(pair) if inward else pair), sems.at[first + i])
            for i, pair in enumerate(ends)
        ]

    arrivals = copies(live, live_far, 0, True)
    arrivals.append(pltpu.make_async_copy(down_far, down, sems.at[2]))
    arrivals.append(pltpu.make_async_copy(lower_far, lower, sems.at[3]))
    later = [pltpu.make_async_copy(x_far, x, sems.at[4]), pltpu.make_async_copy(w_far, w, sems.at[5])]
    for copy in arrivals + later:
        copy.start()
    for copy in arrivals:
        copy.wait()
    upward[...] = nt(down[...], lower[...])
    for copy in later:
        copy.wait()

    @pl.loop(0, 2 * wide // BLOCK)
    def _(t):
        at = tile_rows(t, BLOCK)
        both[:, at] = nn(x[...], w[:, at])

    @pl.loop(0, x.shape[0] // 32)
    def _(i):
        at = tile_rows(i, 32)
        gate, up = both[at, :wide], both[at, wide:]
        alive = live[at, :1]
        grad = upward[at, :] * alive
        sigmoid = 1.0 / (1.0 + jnp.exp(-gate))
        silu = gate * sigmoid
        active_now = silu * up
        active[at, :] = active_now.astype(jnp.bfloat16)
        masked[at, :] = (active_now * alive).astype(jnp.bfloat16)
        gate_grad = grad * up * sigmoid * (1.0 + gate * (1.0 - sigmoid))
        hidden[at, :wide] = gate_grad.astype(jnp.bfloat16)
        hidden[at, wide:] = (grad * silu).astype(jnp.bfloat16)

    leaving = []
    for index, near in enumerate((x, down, masked, hidden)):
        leaving += copies(near, whole[index], 6 + 2 * index, False)
    for copy in leaving:
        copy.start()
    half = x.shape[1] // 2
    for first in (0, half):
        at = pl.ds(first, half)
        back[:, at] = nt(hidden[...], w[at, :]).astype(jnp.bfloat16)
    last = [pltpu.make_async_copy(back, back_far, sems.at[14])]
    last[0].start()
    for first in (0, half):
        at = pl.ds(first, half)
        out[:, at] = nn(active[...], lower[:, at]).astype(jnp.bfloat16)
    last.append(pltpu.make_async_copy(out, out_far, sems.at[15]))
    last[1].start()
    for copy in leaving + last:
        copy.wait()


def dense(chunk, order, x, down, live, w, lower, held):
    rows, features = x.shape
    wide = lower.shape[0]
    slots = 4 * rows
    low_of = lambda *shape: jax.ShapeDtypeStruct(shape, jnp.bfloat16)
    far = pl.BlockSpec(memory_space=pl.ANY)
    keep = lambda *shape: pltpu.VMEM(shape, jnp.bfloat16)
    aliases = {6 + i: i for i in range(len(held))}
    results = pl.pallas_call(
        functools.partial(dense_kernel, chunk, len(held)),
        out_shape=(
            low_of(slots, features), low_of(slots, features), low_of(slots, wide),
            low_of(slots, 2 * wide), low_of(rows, features), low_of(rows, features),
        ),
        in_specs=[SMEM] + [far] * (5 + len(held)),
        out_specs=(far,) * 6,
        scratch_shapes=[
            keep(rows, features), keep(rows, features), pltpu.VMEM((rows, LANES), jnp.float32),
            keep(features, 2 * wide), keep(wide, features),
            pltpu.VMEM((rows, 2 * wide), jnp.float32), pltpu.VMEM((rows, wide), jnp.float32),
            keep(rows, wide), keep(rows, wide), keep(rows, 2 * wide),
            keep(rows, features), keep(rows, features),
            pltpu.SemaphoreType.DMA((16,)),
        ],
        input_output_aliases=aliases,
        compiler_params=pltpu.CompilerParams(vmem_limit_bytes=60 * 2**20),
        name="dense",
    )(order, x, down, live, w, lower, *held)
    return results[5], results[4], results[:4]


LITTLE = pl.CostEstimate(flops=1, bytes_accessed=1, transcendentals=0)
SMEM = pl.BlockSpec(memory_space=pltpu.SMEM)
VMEM = pl.BlockSpec(memory_space=pltpu.VMEM)


def attend_forward(group, qkv, tables, starts, parents, order):
    blocks, block, width = qkv.shape
    slot_count = blocks * block
    wide = pad_lanes(width)
    out_wide = pad_lanes(group * HEAD_DIM)
    live = SEG_TILES * TILE
    return pl.pallas_call(
        functools.partial(forward_kernel, group),
        out_shape=(
            jax.ShapeDtypeStruct((blocks, block, group * HEAD_DIM), jnp.bfloat16),
            jax.ShapeDtypeStruct((group * live, LANES), jnp.bfloat16),
            jax.ShapeDtypeStruct((live, LANES), jnp.bfloat16),
            jax.ShapeDtypeStruct((live, LANES), jnp.bfloat16),
            jax.ShapeDtypeStruct((SEG_TILES, 1, group * TILE), jnp.float32),
        ),
        in_specs=[SMEM, SMEM, SMEM, VMEM, VMEM],
        out_specs=(VMEM,) * 5,
        scratch_shapes=[
            pltpu.VMEM((slot_count + 8, wide), jnp.float32),
            pltpu.VMEM((LANES, live), jnp.bfloat16),
            pltpu.VMEM((slot_count + 8, out_wide), jnp.float32),
        ],
        compiler_params=pltpu.CompilerParams(vmem_limit_bytes=48 * 2**20),
        name="tree_forward",
    )(starts, parents, order, qkv, tables)


def attend_backward(attended_grad, kept, tables, starts, parents, order):
    blocks, block, width = attended_grad.shape
    slot_count = blocks * block
    group = width // HEAD_DIM
    wide = pad_lanes((group + 2) * HEAD_DIM + 2)
    in_wide = pad_lanes(width)
    live = SEG_TILES * TILE
    return pl.pallas_call(
        functools.partial(backward_kernel, group),
        out_shape=jax.ShapeDtypeStruct((blocks, block, wide), jnp.bfloat16),
        in_specs=[SMEM, SMEM, SMEM] + [VMEM] * 6,
        out_specs=VMEM,
        scratch_shapes=[
            pltpu.VMEM((slot_count + 8, in_wide), jnp.float32),
            pltpu.VMEM((group * live, LANES), jnp.bfloat16),
            pltpu.VMEM((LANES, live), jnp.bfloat16),
            pltpu.VMEM((live, LANES), jnp.float32),
            pltpu.VMEM((live, LANES), jnp.float32),
            pltpu.VMEM((live, wide), jnp.float32),
            pltpu.VMEM((slot_count + 8, wide), jnp.float32),
        ],
        compiler_params=pltpu.CompilerParams(vmem_limit_bytes=56 * 2**20),
        cost_estimate=LITTLE,
        name="tree_backward",
    )(starts, parents, order, attended_grad, *kept, tables)


def window(ref, rows, start, size, wide, at):
    full = ref.shape[-1]
    span = min(pad_lanes(size + LANES - 1), full)
    aligned = jnp.minimum(start // LANES * LANES, full - span)
    shift = start - aligned
    values = ref[rows, pl.ds(pl.multiple_of(aligned, LANES), span)].astype(jnp.float32)
    lane = lax.broadcasted_iota(jnp.int32, values.shape, 1)
    values = jnp.where((lane >= shift) & (lane < shift + size), values, 0.0)
    reach = max(span, wide)
    if reach > span:
        filling = jnp.zeros((values.shape[0], reach - span), values.dtype)
        values = jnp.concatenate([values, filling], axis=1)
    return pltpu.roll(values, lax.rem(at - shift + reach, reach), 1)[:, :wide]


def pack_kernel(places, extras, step, spot, *refs):
    sources, gains = refs[: len(places)], refs[len(places) : len(places) + extras]
    pairs = refs[len(places) + extras :]
    half, wide = pairs[0].shape[1:]
    extra_at = sum(size for size, _ in places)

    @pl.loop(0, half // step)
    def _(i):
        rows = pl.ds(pl.multiple_of(spot[1] * half + i * step, step), step)
        there = pl.ds(pl.multiple_of(i * step, step), step)
        lane = lax.broadcasted_iota(jnp.int32, (step, wide), 1)
        for way in range(2 * len(pairs)):
            total = None
            for ref, (size, at) in zip(sources, places):
                part = window(ref, rows, (spot[0] ^ way) * size, size, wide, at)
                total = part if total is None else total + part
            for index, gain in enumerate(gains):
                total = jnp.where(lane == extra_at + index, gain[rows, :].astype(jnp.float32), total)
            pairs[way // 2][way % 2, there, :] = total.astype(jnp.bfloat16)


def pack(weights, gains, spot, places, wide, count, share):
    half = weights[0].shape[0] // share
    return pl.pallas_call(
        functools.partial(pack_kernel, places, len(gains), 16),
        out_shape=(jax.ShapeDtypeStruct((2, half, wide), jnp.bfloat16),) * (count // 2),
        in_specs=[SMEM] + [VMEM] * (len(weights) + len(gains)),
        out_specs=(VMEM,) * (count // 2),
        compiler_params=pltpu.CompilerParams(vmem_limit_bytes=48 * 2**20),
        name="pack_weights",
    )(spot, *weights, *[gain[:, None] for gain in gains])


def assemble_kernel(count, share, extra_at, spot, *refs):
    blocks, mates, whole = refs[: count + share - 1], refs[count + share - 1], refs[count + share]
    rows = mates.shape[1]
    for index in range(share * count):
        turn_of, chip = divmod(index, count)
        for core in range(2):
            slot = spot[0] ^ (2 * chip + core)
            first = slot * (share * rows) + (spot[1] ^ turn_of) * rows
            at = pl.ds(pl.multiple_of(first, 16), rows)
            if core:
                whole[at, :] = mates[index]
            else:
                whole[at, :] = blocks[count][chip, 0] if turn_of else blocks[chip][0]
    if extra_at is not None:
        gains = refs[-1]
        first = extra_at // LANES * LANES
        for index in range(whole.shape[0] // LANES):
            at = pl.ds(index * LANES, LANES)
            part = whole[at, first : first + LANES].astype(jnp.float32).T
            gains[:, at] = pltpu.roll(part, LANES - extra_at % LANES, 0)[:8]


def assemble(pairs, others, spot, extra_at, *waits):
    mates = [jnp.stack([pair[1] for pair in pairs])]
    if others is not None:
        mates.append(others[:, 1])
    mates = swap_core(jnp.concatenate(mates))
    _, rows, wide = pairs[0].shape
    shape = (2 * mates.shape[0] * rows, wide)
    out_shape = (jax.ShapeDtypeStruct(shape, jnp.bfloat16),)
    if extra_at is not None:
        out_shape += (jax.ShapeDtypeStruct((8, shape[0]), jnp.float32),)
    own = pl.BlockSpec((1, rows, wide), lambda i: (0, 0, 0))
    full = lambda *shape: pl.BlockSpec(shape, lambda i: (0,) * len(shape))
    in_specs = [SMEM] + [own] * len(pairs)
    if others is not None:
        in_specs.append(pl.BlockSpec((len(pairs), 1, rows, wide), lambda i: (0, 0, 0, 0)))
    return pl.pallas_call(
        functools.partial(assemble_kernel, len(pairs), 1 if others is None else 2, extra_at),
        grid=(1,),
        out_shape=out_shape,
        in_specs=in_specs + [full(*mates.shape)],
        out_specs=tuple(full(*o.shape) for o in out_shape),
        compiler_params=pltpu.CompilerParams(vmem_limit_bytes=56 * 2**20),
        name="assemble_weights",
    )(spot, *pairs, *([] if others is None else [others]), mates)


def after(values, *earlier):
    anywhere = pl.BlockSpec(memory_space=pl.ANY)
    return pl.pallas_call(
        lambda *refs: None,
        out_shape=tuple(jax.ShapeDtypeStruct(v.shape, v.dtype) for v in values),
        in_specs=[anywhere] * (len(values) + len(earlier)),
        out_specs=(anywhere,) * len(values),
        input_output_aliases={i: i for i in range(len(values))},
        name="after",
    )(*values, *earlier)


def product_kernel(first, index, x, y, *refs):
    out, total = refs[-2:]
    step = pl.program_id(0)

    @pl.when(step == 0)
    def _():
        total[...] = jnp.zeros_like(total)

    total[...] += lax.dot_general(
        x[:, first : first + total.shape[0]], y[...], (((0,), (0,)), ((), ())),
        preferred_element_type=jnp.float32,
    )

    @pl.when(step == pl.num_programs(0) - 1)
    def _():
        out[...] = total[: out.shape[0], :].astype(jnp.bfloat16)


def product(x, y, block, index, first, size, waits):
    rows, wide = y.shape
    step = rows // 4
    held = pad_lanes(size)
    return pl.pallas_call(
        functools.partial(product_kernel, first),
        grid_spec=pltpu.PrefetchScalarGridSpec(
            num_scalar_prefetch=1,
            grid=(4,),
            in_specs=[
                pl.BlockSpec((step, block), lambda k, at: (k, at[0])),
                pl.BlockSpec((step, wide), lambda k, at: (k, 0)),
            ]
            + [pl.BlockSpec(memory_space=pl.ANY)] * len(waits),
            out_specs=pl.BlockSpec((size, wide), lambda k, at: (0, 0)),
            scratch_shapes=[pltpu.VMEM((held, wide), jnp.float32)],
        ),
        out_shape=jax.ShapeDtypeStruct((size, wide), jnp.bfloat16),
        compiler_params=pltpu.CompilerParams(vmem_limit_bytes=48 * 2**20),
        cost_estimate=LITTLE,
        name="product",
    )(index, x, y, *waits)


def spread_kernel(places, count, me, *refs):
    blocks = refs[:count]
    weights = refs[count : count + len(places)]
    outs = refs[count + len(places) : count + 2 * len(places)]
    gain, held = refs[count + 2 * len(places) :]
    for way in range(count):
        held[me[0] ^ way] = blocks[way][...].astype(jnp.float32)
    for out in outs:
        out[...] = jnp.zeros_like(out)
    total = jnp.zeros(gain.shape, jnp.float32)
    for (size, at), weight, out in zip(places, weights, outs):
        full = out.shape[1]
        for index in range(count):
            start = index * size
            span = min(pad_lanes(size + start % LANES), full)
            aligned = min(start // LANES * LANES, full - span)
            shift = start - aligned
            low_lane = at // LANES * LANES
            width = pad_lanes(at - low_lane + size)
            values = held[index][:, low_lane : low_lane + width]
            lane = lax.broadcasted_iota(jnp.int32, values.shape, 1)
            inside = (lane >= at - low_lane) & (lane < at - low_lane + size)
            values = jnp.where(inside, values, 0.0)
            reach = max(span, width)
            if reach > width:
                filling = jnp.zeros((values.shape[0], reach - width), values.dtype)
                values = jnp.concatenate([values, filling], axis=1)
            turned = (shift - (at - low_lane)) % reach
            values = (pltpu.roll(values, turned, 1) if turned else values)[:, :span]
            out[:, aligned : aligned + span] += values
        product = out[...] * weight[...].astype(jnp.float32)
        total = total + jnp.sum(product, axis=1, keepdims=True)
    gain[...] = total


def spread(blocks, weights, me, places, step):
    count = len(blocks)
    rows, wide = weights[0].shape[0], blocks[0].shape[1]
    tile = lambda width: pl.BlockSpec((step, width), lambda i, at: (i, 0))
    block = pl.BlockSpec((step, wide), lambda i, at: (at[0] % 2 * (rows // step) + i, 0))
    return pl.pallas_call(
        functools.partial(spread_kernel, places, count),
        grid_spec=pltpu.PrefetchScalarGridSpec(
            num_scalar_prefetch=1,
            grid=(rows // step,),
            in_specs=[block] * count + [tile(w.shape[1]) for w in weights],
            out_specs=tuple(tile(w.shape[1]) for w in weights) + (tile(1),),
            scratch_shapes=[pltpu.VMEM((count, step, wide), jnp.float32)],
        ),
        out_shape=tuple(jax.ShapeDtypeStruct(w.shape, jnp.float32) for w in weights)
        + (jax.ShapeDtypeStruct((rows, 1), jnp.float32),),
        compiler_params=pltpu.CompilerParams(vmem_limit_bytes=56 * 2**20),
        name="spread_gradients",
    )(me[None].astype(jnp.int32), *blocks, *weights)


def wait(value, *earlier):
    return after((value,), *earlier)[0]


def mark_kernel(*refs):
    refs[-1][...] = jnp.zeros_like(refs[-1])


def flush(*earlier):
    token = pl.pallas_call(
        mark_kernel,
        out_shape=jax.ShapeDtypeStruct((16, LANES), jnp.bfloat16),
        in_specs=[pl.BlockSpec(memory_space=pl.ANY)] * len(earlier),
        out_specs=VMEM,
        name="mark",
    )(*earlier)
    return swap_core(token)


def normed(values):
    inverse = lax.rsqrt(jnp.mean(values * values, axis=-1, keepdims=True) + epsilon)
    return (values * inverse, inverse)


def norm_back(upward, unit_rows, inverse):
    return inverse * (upward - unit_rows * jnp.mean(upward * unit_rows, axis=-1, keepdims=True))


def layout(starts, slot_count):
    slot_index = lax.iota(jnp.int32, slot_count)
    segment_ids = lax.iota(jnp.int32, SEGS)
    segment_len = jnp.where(segment_ids == 0, TRUNK, TILE)
    inside = (slot_index[None, :] >= starts[:, None]) & (
        slot_index[None, :] < (starts + segment_len)[:, None]
    )
    return jnp.any(inside, axis=0)


def dot(left, right):
    return jnp.dot(left, right, preferred_element_type=jnp.float32)


def transpose_dot(left, right):
    return lax.dot_general(
        left, right, (((1,), (1,)), ((), ())), preferred_element_type=jnp.float32
    )


def rows_dot(left, right):
    return lax.dot_general(
        left, right, (((0,), (0,)), ((), ())), preferred_element_type=jnp.float32
    )


def low(values):
    return values.astype(jnp.bfloat16)


def plain(count):
    return count != 8 or lax.axis_size("replica") != 4


def gather_order(count):
    if plain(count):
        return [list(range(count))] * count
    ways = ((0, 1, 2, 3, 5, 4, 6, 7), (0, 1, 4, 5, 3, 2, 6, 7))
    return [[index ^ way for way in ways[index % 2]] for index in range(count)]


def swap_core(values):
    return lax.ppermute(values, "slot", [(i, i ^ 1) for i in range(8)])


def swap_near(values):
    return lax.ppermute(values, "slot", [(i, i ^ (4 if i % 2 else 2)) for i in range(8)])


def swap_far(values):
    return lax.ppermute(values, "slot", [(i, i ^ (2 if i % 2 else 4)) for i in range(8)])


def gather(own):
    count = lax.axis_size("slot")
    if plain(count):
        return jnp.split(lax.all_gather(own, "slot", axis=0, tiled=True), 4, axis=0)
    block = own.shape[0]
    chip = jnp.concatenate([own, swap_core(own)], axis=0)
    near = swap_near(chip)
    corner = swap_far(near[:block])
    return [chip, near, swap_core(near), jnp.concatenate([corner, swap_core(corner)], axis=0)]


def scatter(parts, *between):
    count = lax.axis_size("slot")
    if plain(count):
        whole = jnp.concatenate(parts, axis=0)
        return lax.psum_scatter(whole, "slot", scatter_dimension=0, tiled=True).astype(
            jnp.float32
        )
    chip, near, side, corner = parts
    block = chip.shape[0] // 2
    wide = lambda values: values.astype(jnp.float32)
    near_sum = low(wide(near) + wide(swap_core(side)))
    corner_sum = low(wide(corner[:block]) + wide(swap_core(corner[block:])))
    arrived = swap_far(corner_sum), swap_near(near_sum[block:])
    if between:
        arrived = after(arrived, *between[0](corner_sum))
    near_own = low(wide(near_sum[:block]) + wide(arrived[0]))
    other = low(wide(chip[block:]) + wide(arrived[1]))
    arrived = swap_near(near_own), swap_core(other)
    if between:
        arrived = after(arrived, *between[1](near_own))
    return wide(chip[:block]) + wide(arrived[0]) + wide(arrived[1])


def send(block, way):
    count = lax.axis_size("slot")
    if way == 0:
        return block
    return lax.ppermute(block, "slot", [(i, i ^ way) for i in range(count)])


def sum_trees(part):
    return lax.psum(part, "replica")


def plain_columns(weights, gains, places, wide, heads_in):
    count = lax.axis_size("slot")
    extra_at = sum(size for size, _ in places)
    blocks = jnp.zeros((count, weights[0].shape[0], wide), jnp.bfloat16)
    for weight, (size, at), heads in zip(weights, places, heads_in):
        blocks = blocks.at[:, :, at : at + size].set(split_columns(weight, count, heads))
    for index, gain in enumerate(gains):
        blocks = blocks.at[:, :, extra_at + index].set(gain[None])
    whole = lax.all_to_all(blocks, "slot", 0, 0).reshape(-1, wide)
    return whole, whole[:, extra_at : extra_at + len(gains)].T.astype(jnp.float32)


def send_pairs(pairs):
    return [send(pair, 2 * chip) for chip, pair in enumerate(pairs)]


def swap_halves(pairs):
    trees = lax.axis_size("replica")
    return lax.ppermute(pairs, "replica", [(i, i ^ 1) for i in range(trees)])


def plain_rows(gradient, weights, places, heads_in):
    count = lax.axis_size("slot")
    rows = gradient.shape[0] // count
    blocks = lax.all_to_all(gradient.reshape(count, rows, -1), "slot", 0, 0)
    blocks = sum_trees(blocks).astype(jnp.float32)
    parts = [
        join_columns(blocks[:, :, at : at + size], heads)
        for (size, at), heads in zip(places, heads_in)
    ]
    products = [jnp.sum(p * w.astype(jnp.float32), axis=1) for p, w in zip(parts, weights)]
    return parts, sum(products)


def split_columns(weight, count, heads_in=None):
    rows, columns = weight.shape
    if heads_in is not None and heads_in < count:
        weight = weight.reshape(rows, heads_in, columns // heads_in)
        weight = jnp.repeat(weight, count // heads_in, axis=1)
    else:
        weight = weight.reshape(rows, count, columns // count)
    return weight.transpose(1, 0, 2)


def join_columns(blocks, heads_in=None):
    count, rows, columns = blocks.shape
    if heads_in is not None and heads_in < count:
        blocks = jnp.sum(blocks.reshape(heads_in, count // heads_in, rows, columns), axis=1)
        count = heads_in
    return blocks.transpose(1, 0, 2).reshape(rows, count * columns)


def shards(
    layer_in,
    seg_starts,
    seg_parents,
    w_query,
    w_key,
    w_value,
    w_out,
    w_gate,
    w_up,
    w_down,
    gain_attn,
    gain_ffn,
    out_cotangent,
):
    count = lax.axis_size("slot")
    me = lax.axis_index("slot")
    row_count = layer_in.shape[1]
    slot_count = row_count * count
    features = layer_in.shape[2]
    kv_heads = w_key.shape[1] // HEAD_DIM
    q_width = w_query.shape[1] // count
    heads_width = q_width + 2 * HEAD_DIM
    heads_wide = pad_lanes(heads_width + 2)
    hidden = w_down.shape[0]
    hidden_wide = pad_lanes(hidden)
    starts, parents = seg_starts[0], seg_parents[0]
    tile_starts = jnp.concatenate([lax.iota(jnp.int32, TRUNK_TILES) * TILE, starts[1:]])
    order = jnp.asarray(gather_order(count), jnp.int32)[me]
    tables = turn_tables()
    live = layout(starts, slot_count).astype(jnp.float32).reshape(count, row_count)
    my_live = live[me]

    def cut(values):
        return jnp.split(values, 4, axis=0)

    def blocks_of(parts):
        return jnp.concatenate(parts, axis=0).reshape(count, row_count, parts[0].shape[-1])

    special = not plain(count)
    head_weights = (w_query, w_key, w_value)
    head_places = ((q_width, 0), (HEAD_DIM, q_width), (HEAD_DIM, q_width + HEAD_DIM))
    head_counts = (None, kv_heads, kv_heads)
    hidden_places = ((hidden, 0), (hidden, hidden_wide))
    gain_pair = (gain_attn, gain_ffn)

    def attn_part(part):
        return low(normed(part.astype(jnp.float32))[0] * full_gain_attn)

    if special:
        flat = jnp.stack([me, jnp.zeros_like(me)]).astype(jnp.int32)
        chip = jnp.concatenate([layer_in[0], swap_core(layer_in[0])], axis=0)
        near = swap_near(chip)
        packed = pack(head_weights, gain_pair, flat, head_places, heads_wide, count, 1)
        hidden_packed = pack((w_gate, w_up), (), flat, hidden_places, 2 * hidden_wide, count, 1)
        head_pairs = send_pairs(packed)
        head_pairs = after(head_pairs, flush(hidden_packed[0]))
        w_heads, gains = assemble(head_pairs, None, flat, heads_width)
        full_gain_attn, full_gain_ffn = gains[0], gains[1]
        near = wait(near, head_pairs[1])
        corner, side = swap_far(near[:row_count]), swap_core(near)
        hidden_pairs = send_pairs(after(hidden_packed, near))
        token = flush(near)
        attn_parts = [attn_part(part) for part in (wait(chip, token), near, side)]
        parts = [dot(part, w_heads) for part in attn_parts]
        corner = jnp.concatenate([corner, swap_core(corner)], axis=0)
        attn_parts.append(attn_part(corner))
        parts.append(dot(attn_parts[3], w_heads))
        qkv = blocks_of(parts)
    else:
        layer_parts = gather(layer_in[0])
        w_heads, gains = plain_columns(
            head_weights, gain_pair, head_places, heads_wide, head_counts
        )
        w_hidden, _ = plain_columns(
            (w_gate, w_up), (), hidden_places, 2 * hidden_wide, (None, None)
        )
        full_gain_attn, full_gain_ffn = gains[0], gains[1]
        attn_parts = [attn_part(part) for part in layer_parts]
        qkv = blocks_of([dot(part, w_heads) for part in attn_parts])
    attended, *kept = attend_forward(q_width // HEAD_DIM, qkv, tables, tile_starts, parents, order)
    attended = attended.reshape(slot_count, q_width)
    if special:
        hidden_pairs = after(hidden_pairs, attended)
        (w_hidden,) = assemble(hidden_pairs, None, flat, None)
        attended = wait(attended, hidden_pairs[1])
    residual = layer_in[0].astype(jnp.float32)
    middle = residual + scatter([low(dot(part, w_out)) for part in cut(attended)])

    w_lower = jnp.pad(w_down, ((0, hidden_wide - hidden), (0, 0)))
    live_rows = jnp.broadcast_to(live.reshape(slot_count, 1), (slot_count, LANES))
    unit_ffn, rms_ffn = normed(middle)
    ffn_input = low(unit_ffn * full_gain_ffn)
    if special:
        feed = lambda index, part, down, held: dense(
            index, order, part, down, live_rows, w_hidden, w_lower, held
        )
        both = jnp.stack([ffn_input, wait(out_cotangent[0], attended)])
        chip_both = jnp.concatenate([both, swap_core(both)], axis=1)
        near_part, near_down = swap_near(chip_both[0]), swap_near(chip_both[1])
        chip_back, chip_out, held = feed(0, chip_both[0], chip_both[1], ())
        near_part = wait(near_part, chip_back)
        near_down = wait(near_down, chip_back)
        corner, corner_down = swap_far(near_part[:row_count]), swap_far(near_down[:row_count])
        side_part, side_down = swap_core(near_part), swap_core(near_down)
        near_back, near_out, held = feed(1, near_part, near_down, held)
        side_back, side_out, held = feed(2, side_part, side_down, held)
        corner, corner_down = after((corner, corner_down), near_back)
        corner_part = jnp.concatenate([corner, swap_core(corner)], axis=0)
        corner_down = jnp.concatenate([corner_down, swap_core(corner_down)], axis=0)
        corner_back, corner_out, held = feed(3, corner_part, corner_down, held)
        back_parts = [chip_back, near_back, side_back, corner_back]
        out_parts = [chip_out, near_out, side_out, corner_out]
    else:
        held, back_parts, out_parts = (), [], []
        pairs = zip(gather(ffn_input), gather(out_cotangent[0]))
        for index, (part, down) in enumerate(pairs):
            back, out, held = dense(
                index, lax.iota(jnp.int32, 4), part, down, live_rows, w_hidden, w_lower, held
            )
            back_parts.append(back)
            out_parts.append(out)
    ffn_rows, down_rows, active_rows, hidden_rows = held
    upstream = out_cotangent[0].astype(jnp.float32) * my_live[:, None]

    def middle_of(ffn_input_grad):
        return upstream + norm_back(ffn_input_grad * full_gain_ffn, unit_ffn, rms_ffn)

    def hidden_part(chip, *waits):
        span = 2 * features // count
        index = ((me ^ chip) // 2)[None].astype(jnp.int32)
        return product(ffn_rows, hidden_rows, span, index, 0, span, waits)

    def to_heads(part):
        return low(transpose_dot(part, w_out))

    def proj_part():
        return low(sum(rows_dot(a, b) for a, b in zip(cut(attended), branch_parts)))

    def heads_part():
        return low(sum(rows_dot(a, b) for a, b in zip(attn_parts, head_parts)))

    if special:
        hidden_parts = []

        def all_hidden(mark):
            for chip in (0, 2, 4, 6):
                hidden_parts.append(hidden_part(chip, mark, *hidden_parts[-1:]))
            return hidden_parts[-1:]

        ffn_input_grad = scatter(back_parts, all_hidden, lambda mark: (mark,))
        middle_grad = middle_of(ffn_input_grad)
        branch = low(middle_grad)
        chip_part = jnp.concatenate([branch, swap_core(branch)], axis=0)
        near_part = swap_near(chip_part)
        hidden_sums = lax.psum(tuple(hidden_parts), "replica")
        side_part = swap_core(near_part)
        corner = swap_far(near_part[:row_count])
        index = jnp.zeros((1,), jnp.int32)
        grad_down = product(active_rows, down_rows, hidden_wide, index, 0, hidden, (chip_part,))
        corner = wait(corner, grad_down)
        corner_part = jnp.concatenate([corner, swap_core(corner)], axis=0)
        branch_parts = [chip_part, near_part, side_part, corner_part]
    else:
        middle_grad = middle_of(scatter(back_parts))
        branch_parts = gather(low(middle_grad))
    attended_grad = blocks_of([to_heads(part) for part in branch_parts])
    head_grads = attend_backward(attended_grad, kept, tables, tile_starts, parents, order)
    head_parts = cut(head_grads.reshape(slot_count, heads_wide))
    input_parts = [low(transpose_dot(part, w_heads)) for part in head_parts]
    attn_input_grad = scatter(input_parts)
    unit_attn, rms_attn = normed(residual)
    grad_in = low(
        middle_grad + norm_back(attn_input_grad * full_gain_attn, unit_attn, rms_attn)
    )
    grad_proj, grad_heads = proj_part(), heads_part()
    if special:
        out_parts = after(out_parts, grad_in)
    layer_out = low(middle + scatter(out_parts))

    if special:

        def settled(sums):
            blocks = []
            for chip, summed in zip(range(0, count, 2), sums):
                block = send(summed, chip)
                blocks += [block, swap_core(block)]
            return blocks

        hidden_sums = after(hidden_sums, grad_in, grad_heads, grad_proj)
        grad_heads, grad_proj = after((grad_heads, grad_proj), *hidden_sums)
        grad_heads, grad_proj = lax.psum((grad_heads, grad_proj), "replica")
        blocks = settled(hidden_sums)
        grad_gate, grad_up, gain_ffn_sum = spread(blocks, (w_gate, w_up), me, hidden_places, 32)
        grad_heads, grad_proj = after((grad_heads, grad_proj), grad_gate)
        grad_down = lax.psum(wait(grad_down, grad_heads), "replica")
        span = 2 * features // count
        blocks = settled(
            [
                lax.dynamic_slice_in_dim(grad_heads, (me ^ chip) // 2 * span, span)
                for chip in range(0, count, 2)
            ]
        )
        grad_query, grad_key, grad_value, gain_attn_sum = spread(
            blocks, head_weights, me, head_places, 64
        )
        gain_ffn_sum, gain_attn_sum = gain_ffn_sum[:, 0], gain_attn_sum[:, 0]
        grad_down = wait(grad_down, grad_query)
    else:
        grad_down = sum_trees(low(rows_dot(active_rows, down_rows)[:hidden]))
        (grad_gate, grad_up), gain_ffn_sum = plain_rows(
            low(rows_dot(ffn_rows, hidden_rows)), (w_gate, w_up), hidden_places, (None, None)
        )
        grad_proj = sum_trees(grad_proj)
        (grad_query, grad_key, grad_value), gain_attn_sum = plain_rows(
            grad_heads, head_weights, head_places, head_counts
        )
    return (
        layer_out[None],
        grad_in[None],
        grad_query,
        grad_key,
        grad_value,
        grad_proj.astype(jnp.float32),
        grad_gate,
        grad_up,
        grad_down.astype(jnp.float32),
        gain_attn_sum / gain_attn.astype(jnp.float32),
        gain_ffn_sum / gain_ffn.astype(jnp.float32),
    )


def solution(mesh):
    tokens, tree, rows, vector = P("replica", "slot", None), P("replica", None), P("slot", None), P("slot")
    in_specs = (tokens, tree, tree) + (rows,) * 7 + (vector, vector, tokens)
    out_specs = (tokens, tokens) + (rows,) * 7 + (vector, vector)
    return jax.shard_map(shards, mesh=mesh, in_specs=in_specs, out_specs=out_specs, check_vma=False)
```

```python
import functools
import jax
import jax.numpy as jnp
from jax import lax
from jax.experimental import pallas as pl
from jax.experimental.pallas import tpu as pltpu
from jax.sharding import PartitionSpec as P

HEAD_DIM = 80
TRUNK = 768
SEGS = 13
TILE = 128
NBRANCH = 4
SEG_TILES = TRUNK // TILE + SEGS - 1
TRUNK_TILES = TRUNK // TILE
LANES = 128
BLOCK = 256
epsilon = 1e-05
masked_score = -1e30
rope_theta = 10000.0
log2e = 1.4426950408889634


def pad_lanes(width):
    return -(-width // LANES) * LANES


def turn_tables():
    half = HEAD_DIM // 2
    frequency = jnp.power(rope_theta, -2.0 * lax.iota(jnp.float32, half) / HEAD_DIM)
    angle = lax.iota(jnp.float32, TRUNK + 2 * TILE)[:, None] * frequency[None, :]
    cosine, sine = jnp.cos(angle), jnp.sin(angle)
    none = jnp.zeros_like(sine)
    tail = jnp.zeros((angle.shape[0], LANES - HEAD_DIM), jnp.float32)
    return jnp.stack(
        [
            jnp.concatenate([cosine, cosine, tail], axis=1),
            jnp.concatenate([none, sine, tail], axis=1),
            jnp.concatenate([-sine, none, tail], axis=1),
        ]
    )


def tile_base(tile):
    return jnp.where(
        tile < TRUNK_TILES,
        tile * TILE,
        jnp.where(tile < TRUNK_TILES + NBRANCH, TRUNK, TRUNK + TILE),
    )


def take_head(rows, head):
    width = rows.shape[1]
    shift = (width - head * HEAD_DIM) % width
    return (pltpu.roll(rows, shift, 1) if shift else rows)[:, :LANES]


def put_head(part, head, width):
    wide = jnp.concatenate(
        [part, jnp.zeros((part.shape[0], width - LANES), part.dtype)], axis=1
    )
    return pltpu.roll(wide, head * HEAD_DIM, 1) if head else wide


def turn(rows, tables, sign):
    half = HEAD_DIM // 2
    cosine, up, down = tables
    swapped = pltpu.roll(rows, half, 1) * up + pltpu.roll(rows, LANES - half, 1) * down
    return rows * cosine + swapped if sign > 0 else rows * cosine - swapped


def head_lanes(rows):
    lane = lax.broadcasted_iota(jnp.int32, rows.shape, 1)
    return jnp.where(lane < HEAD_DIM, rows, 0.0)


def read_rows(ref, start):
    aligned = pl.multiple_of(start // 8 * 8, 8)
    rows = ref[pl.ds(aligned, TILE + 8), :]
    return pltpu.roll(rows, (TILE + 8) - (start - aligned), 0)[:TILE]


def write_rows(ref, start, rows):
    aligned = pl.multiple_of(start // 8 * 8, 8)
    offset = start - aligned
    at = pl.ds(aligned, TILE + 8)
    wide = jnp.concatenate([rows, jnp.zeros((8, rows.shape[1]), rows.dtype)], axis=0)
    wide = pltpu.roll(wide, offset, 0)
    index = lax.broadcasted_iota(jnp.int32, wide.shape, 0)
    inside = (index >= offset) & (index < offset + TILE)
    ref[at, :] = jnp.where(inside, wide, ref[at, :])


def nt(a, b):
    return lax.dot_general(a, b, (((1,), (1,)), ((), ())), preferred_element_type=jnp.float32)


def nn(a, b):
    return lax.dot_general(a, b, (((1,), (0,)), ((), ())), preferred_element_type=jnp.float32)


def causal(columns):
    key = lax.broadcasted_iota(jnp.int32, (TILE, columns), 0)
    query = lax.broadcasted_iota(jnp.int32, (TILE, columns), 1) % TILE
    return key <= query


def each_tile(tile_fn, parent_of):
    for tile in range(TRUNK_TILES):
        tile_fn(tile, tile * TILE, None)

    @pl.loop(TRUNK_TILES, TRUNK_TILES + NBRANCH)
    def _(tile):
        tile_fn(tile, TRUNK, None)

    @pl.loop(TRUNK_TILES + NBRANCH, SEG_TILES)
    def _(tile):
        tile_fn(tile, TRUNK, parent_of(tile) + TRUNK_TILES - 1)


def tile_rows(tile, size=TILE):
    if isinstance(tile, int):
        return pl.ds(tile * size, size)
    return pl.ds(pl.multiple_of(tile * size, size), size)


def forward_kernel(
    group, starts, parents, order, qkv, tables,
    attended, q_keep, k_keep, v_keep, lse_keep,
    slots, v_turned, out_rows,
):
    slot_count = qkv.shape[0] * qkv.shape[1]
    width = slots.shape[1]
    out_width = out_rows.shape[1]
    block = qkv.shape[1]

    @pl.loop(0, qkv.shape[0])
    def _(i):
        slots[pl.ds(pl.multiple_of(order[i] * block, 8), block), :] = qkv[i]

    @pl.loop(0, slot_count // TILE)
    def _(i):
        rows = tile_rows(i)
        own = take_head(slots[rows, :], group + 1)
        own = head_lanes(own).astype(jnp.bfloat16).astype(jnp.float32)
        total = put_head(own, 0, out_width)
        for head in range(1, group):
            total = total + put_head(own, head, out_width)
        out_rows[rows, :] = total

    @pl.loop(0, SEG_TILES)
    def _(tile):
        rows = read_rows(slots, starts[tile])
        base = pl.ds(pl.multiple_of(tile_base(tile), TILE), TILE)
        turns = tuple(tables[t, base, :] for t in range(3))
        for head in range(group):
            turned = turn(take_head(rows, head), turns, 1) * (HEAD_DIM**-0.5 * log2e)
            at = pl.ds(pl.multiple_of(tile * (group * TILE) + head * TILE, TILE), TILE)
            q_keep[at, :] = turned.astype(jnp.bfloat16)
        k_keep[tile_rows(tile), :] = turn(take_head(rows, group), turns, 1).astype(jnp.bfloat16)
        own = head_lanes(take_head(rows, group + 1))
        v_keep[tile_rows(tile), :] = own.astype(jnp.bfloat16)
        v_turned[:, tile_rows(tile)] = own.T.astype(jnp.bfloat16)

    columns = group * TILE

    def attend(tile, full, parent):
        queries = q_keep[tile_rows(tile, columns), :]
        keys = [pl.ds(0, full)] if full else []
        if parent is not None:
            keys.append(tile_rows(parent))
        keys.append(tile_rows(tile))
        scores = [nt(k_keep[at, :], queries) for at in keys]
        scores[-1] = jnp.where(causal(columns), scores[-1], masked_score)
        top = functools.reduce(jnp.maximum, [jnp.max(s, axis=0, keepdims=True) for s in scores])
        weights = [jnp.exp2(s - top) for s in scores]
        total = functools.reduce(jnp.add, [jnp.sum(w, axis=0, keepdims=True) for w in weights])
        mixed = functools.reduce(
            jnp.add,
            [nn(v_turned[:, at], w.astype(jnp.bfloat16)) for at, w in zip(keys, weights)],
        )
        mixed = mixed * (1.0 / total)
        lse_keep[pl.ds(tile, 1)] = (top + jnp.log2(total))[None]
        result = put_head(mixed[:, :TILE].T, 0, out_width)
        for head in range(1, group):
            result = result + put_head(
                mixed[:, head * TILE : (head + 1) * TILE].T, head, out_width
            )
        write_rows(out_rows, starts[tile], result)

    each_tile(attend, lambda tile: parents[tile - TRUNK_TILES + 1])

    kept = attended.shape[-1]

    @pl.loop(0, qkv.shape[0])
    def _(i):
        rows = out_rows[pl.ds(pl.multiple_of(order[i] * block, 8), block), :]
        attended[i] = rows[:, :kept].astype(jnp.bfloat16)


def backward_kernel(
    group, starts, parents, order, attended_grad, q_keep, k_keep, v_keep, lse_keep, tables,
    grads,
    slots, do_keep, k_turned, dk, dv, dq, out_rows,
):
    slot_count = attended_grad.shape[0] * attended_grad.shape[1]
    in_width = slots.shape[1]
    width = out_rows.shape[1]
    block = attended_grad.shape[1]
    kept = attended_grad.shape[2]
    columns = group * TILE

    slots[...] = jnp.zeros_like(slots)

    @pl.loop(0, attended_grad.shape[0])
    def _(i):
        at = pl.ds(pl.multiple_of(order[i] * block, 8), block)
        slots[at, :kept] = attended_grad[i].astype(jnp.float32)

    @pl.loop(0, slot_count // TILE)
    def _(i):
        rows = slots[tile_rows(i), :]
        total = take_head(rows, 0)
        for head in range(1, group):
            total = total + take_head(rows, head)
        out_rows[tile_rows(i), :] = put_head(head_lanes(total), group + 1, width)

    @pl.loop(0, SEG_TILES)
    def _(tile):
        rows = read_rows(slots, starts[tile])
        for head in range(group):
            at = pl.ds(pl.multiple_of(tile * columns + head * TILE, TILE), TILE)
            do_keep[at, :] = head_lanes(take_head(rows, head)).astype(jnp.bfloat16)
        k_turned[:, tile_rows(tile)] = (
            k_keep[tile_rows(tile), :].astype(jnp.float32).T.astype(jnp.bfloat16)
        )

    dk[...] = jnp.zeros_like(dk)
    dv[...] = jnp.zeros_like(dv)

    def attend(tile, full, parent):
        queries = q_keep[tile_rows(tile, columns), :]
        upward = do_keep[tile_rows(tile, columns), :]
        lse = lse_keep[pl.ds(tile, 1)][0]
        keys = [pl.ds(0, full)] if full else []
        if parent is not None:
            keys.append(tile_rows(parent))
        keys.append(tile_rows(tile))
        probs = [jnp.exp2(nt(k_keep[at, :], queries) - lse) for at in keys]
        probs[-1] = jnp.where(causal(columns), probs[-1], 0.0)
        prob_grads = [nt(v_keep[at, :], upward) for at in keys]
        row_dot = functools.reduce(
            jnp.add,
            [jnp.sum(p * g, axis=0, keepdims=True) for p, g in zip(probs, prob_grads)],
        )
        mixed = None
        for at, p, g in zip(keys, probs, prob_grads):
            score_grad = (p * (g - row_dot)).astype(jnp.bfloat16)
            dv[at, :] += nn(p.astype(jnp.bfloat16), upward)
            dk[at, :] += nn(score_grad, queries)
            part = nn(k_turned[:, at], score_grad)
            mixed = part if mixed is None else mixed + part
        base = pl.ds(pl.multiple_of(tile_base(tile), TILE), TILE)
        turns = tuple(tables[t, base, :] for t in range(3))
        result = None
        for head in range(group):
            part = turn(mixed[:, head * TILE : (head + 1) * TILE].T, turns, -1) * HEAD_DIM**-0.5
            part = put_head(part, head, width)
            result = part if result is None else result + part
        dq[tile_rows(tile), :] = result

    each_tile(attend, lambda tile: parents[tile - TRUNK_TILES + 1])

    @pl.loop(0, SEG_TILES)
    def _(tile):
        rows = tile_rows(tile)
        base = pl.ds(pl.multiple_of(tile_base(tile), TILE), TILE)
        turns = tuple(tables[t, base, :] for t in range(3))
        key_part = turn(dk[rows, :], turns, -1) * (1.0 / log2e)
        total = dq[rows, :] + put_head(key_part, group, width)
        total = total + put_head(dv[rows, :], group + 1, width)
        write_rows(out_rows, starts[tile], total)

    @pl.loop(0, attended_grad.shape[0])
    def _(i):
        rows = out_rows[pl.ds(pl.multiple_of(order[i] * block, 8), block), :]
        grads[i] = rows[:, : grads.shape[2]].astype(jnp.bfloat16)


def dense_kernel(
    chunk, held, order, x_far, down_far, live_far, w_far, lower_far, *refs
):
    refs = refs[held:]
    whole, out_far, back_far, refs = refs[:4], refs[4], refs[5], refs[6:]
    x, down, live, w, lower, both, upward, active, masked, hidden, back, out, sems = refs
    wide = lower.shape[0]
    blocks = order.shape[0] // 4
    block = x.shape[0] // blocks
    inside = [pl.ds(i * block, block) for i in range(blocks)]
    rows = [
        pl.ds(pl.multiple_of(order[chunk * blocks + i] * block, 16), block) for i in range(blocks)
    ]

    def copies(near, far, first, inward):
        ends = [(near.at[a], far.at[b]) for a, b in zip(inside, rows)]
        return [
            pltpu.make_async_copy(*(reversed(pair) if inward else pair), sems.at[first + i])
            for i, pair in enumerate(ends)
        ]

    arrivals = copies(live, live_far, 0, True)
    arrivals.append(pltpu.make_async_copy(down_far, down, sems.at[2]))
    arrivals.append(pltpu.make_async_copy(lower_far, lower, sems.at[3]))
    later = [pltpu.make_async_copy(x_far, x, sems.at[4]), pltpu.make_async_copy(w_far, w, sems.at[5])]
    for copy in arrivals + later:
        copy.start()
    for copy in arrivals:
        copy.wait()
    upward[...] = nt(down[...], lower[...])
    for copy in later:
        copy.wait()

    @pl.loop(0, 2 * wide // BLOCK)
    def _(t):
        at = tile_rows(t, BLOCK)
        both[:, at] = nn(x[...], w[:, at])

    @pl.loop(0, x.shape[0] // 32)
    def _(i):
        at = tile_rows(i, 32)
        gate, up = both[at, :wide], both[at, wide:]
        alive = live[at, :1]
        grad = upward[at, :] * alive
        sigmoid = 1.0 / (1.0 + jnp.exp(-gate))
        silu = gate * sigmoid
        active_now = silu * up
        active[at, :] = active_now.astype(jnp.bfloat16)
        masked[at, :] = (active_now * alive).astype(jnp.bfloat16)
        gate_grad = grad * up * sigmoid * (1.0 + gate * (1.0 - sigmoid))
        hidden[at, :wide] = gate_grad.astype(jnp.bfloat16)
        hidden[at, wide:] = (grad * silu).astype(jnp.bfloat16)

    leaving = []
    for index, near in enumerate((x, down, masked, hidden)):
        leaving += copies(near, whole[index], 6 + 2 * index, False)
    for copy in leaving:
        copy.start()
    half = x.shape[1] // 2
    for first in (0, half):
        at = pl.ds(first, half)
        back[:, at] = nt(hidden[...], w[at, :]).astype(jnp.bfloat16)
    last = [pltpu.make_async_copy(back, back_far, sems.at[14])]
    last[0].start()
    for first in (0, half):
        at = pl.ds(first, half)
        out[:, at] = nn(active[...], lower[:, at]).astype(jnp.bfloat16)
    last.append(pltpu.make_async_copy(out, out_far, sems.at[15]))
    last[1].start()
    for copy in leaving + last:
        copy.wait()


def dense(chunk, order, x, down, live, w, lower, held):
    rows, features = x.shape
    wide = lower.shape[0]
    slots = 4 * rows
    low_of = lambda *shape: jax.ShapeDtypeStruct(shape, jnp.bfloat16)
    far = pl.BlockSpec(memory_space=pl.ANY)
    keep = lambda *shape: pltpu.VMEM(shape, jnp.bfloat16)
    aliases = {6 + i: i for i in range(len(held))}
    results = pl.pallas_call(
        functools.partial(dense_kernel, chunk, len(held)),
        out_shape=(
            low_of(slots, features), low_of(slots, features), low_of(slots, wide),
            low_of(slots, 2 * wide), low_of(rows, features), low_of(rows, features),
        ),
        in_specs=[SMEM] + [far] * (5 + len(held)),
        out_specs=(far,) * 6,
        scratch_shapes=[
            keep(rows, features), keep(rows, features), pltpu.VMEM((rows, LANES), jnp.float32),
            keep(features, 2 * wide), keep(wide, features),
            pltpu.VMEM((rows, 2 * wide), jnp.float32), pltpu.VMEM((rows, wide), jnp.float32),
            keep(rows, wide), keep(rows, wide), keep(rows, 2 * wide),
            keep(rows, features), keep(rows, features),
            pltpu.SemaphoreType.DMA((16,)),
        ],
        input_output_aliases=aliases,
        compiler_params=pltpu.CompilerParams(vmem_limit_bytes=60 * 2**20),
        name="dense",
    )(order, x, down, live, w, lower, *held)
    return results[5], results[4], results[:4]


LITTLE = pl.CostEstimate(flops=1, bytes_accessed=1, transcendentals=0)
SMEM = pl.BlockSpec(memory_space=pltpu.SMEM)
VMEM = pl.BlockSpec(memory_space=pltpu.VMEM)


def attend_forward(group, qkv, tables, starts, parents, order):
    blocks, block, width = qkv.shape
    slot_count = blocks * block
    wide = pad_lanes(width)
    out_wide = pad_lanes(group * HEAD_DIM)
    live = SEG_TILES * TILE
    return pl.pallas_call(
        functools.partial(forward_kernel, group),
        out_shape=(
            jax.ShapeDtypeStruct((blocks, block, group * HEAD_DIM), jnp.bfloat16),
            jax.ShapeDtypeStruct((group * live, LANES), jnp.bfloat16),
            jax.ShapeDtypeStruct((live, LANES), jnp.bfloat16),
            jax.ShapeDtypeStruct((live, LANES), jnp.bfloat16),
            jax.ShapeDtypeStruct((SEG_TILES, 1, group * TILE), jnp.float32),
        ),
        in_specs=[SMEM, SMEM, SMEM, VMEM, VMEM],
        out_specs=(VMEM,) * 5,
        scratch_shapes=[
            pltpu.VMEM((slot_count + 8, wide), jnp.float32),
            pltpu.VMEM((LANES, live), jnp.bfloat16),
            pltpu.VMEM((slot_count + 8, out_wide), jnp.float32),
        ],
        compiler_params=pltpu.CompilerParams(vmem_limit_bytes=48 * 2**20),
        name="tree_forward",
    )(starts, parents, order, qkv, tables)


def attend_backward(attended_grad, kept, tables, starts, parents, order):
    blocks, block, width = attended_grad.shape
    slot_count = blocks * block
    group = width // HEAD_DIM
    wide = pad_lanes((group + 2) * HEAD_DIM + 2)
    in_wide = pad_lanes(width)
    live = SEG_TILES * TILE
    return pl.pallas_call(
        functools.partial(backward_kernel, group),
        out_shape=jax.ShapeDtypeStruct((blocks, block, wide), jnp.bfloat16),
        in_specs=[SMEM, SMEM, SMEM] + [VMEM] * 6,
        out_specs=VMEM,
        scratch_shapes=[
            pltpu.VMEM((slot_count + 8, in_wide), jnp.float32),
            pltpu.VMEM((group * live, LANES), jnp.bfloat16),
            pltpu.VMEM((LANES, live), jnp.bfloat16),
            pltpu.VMEM((live, LANES), jnp.float32),
            pltpu.VMEM((live, LANES), jnp.float32),
            pltpu.VMEM((live, wide), jnp.float32),
            pltpu.VMEM((slot_count + 8, wide), jnp.float32),
        ],
        compiler_params=pltpu.CompilerParams(vmem_limit_bytes=56 * 2**20),
        cost_estimate=LITTLE,
        name="tree_backward",
    )(starts, parents, order, attended_grad, *kept, tables)


def window(ref, rows, start, size, wide, at):
    full = ref.shape[-1]
    span = min(pad_lanes(size + LANES - 1), full)
    aligned = jnp.minimum(start // LANES * LANES, full - span)
    shift = start - aligned
    values = ref[rows, pl.ds(pl.multiple_of(aligned, LANES), span)].astype(jnp.float32)
    lane = lax.broadcasted_iota(jnp.int32, values.shape, 1)
    values = jnp.where((lane >= shift) & (lane < shift + size), values, 0.0)
    reach = max(span, wide)
    if reach > span:
        filling = jnp.zeros((values.shape[0], reach - span), values.dtype)
        values = jnp.concatenate([values, filling], axis=1)
    return pltpu.roll(values, lax.rem(at - shift + reach, reach), 1)[:, :wide]


def pack_kernel(places, extras, step, chips, spot, *refs):
    sources, gains = refs[: len(places)], refs[len(places) : len(places) + extras]
    pairs = refs[len(places) + extras :]
    half, wide = pairs[0].shape[1:]
    extra_at = sum(size for size, _ in places)

    @pl.loop(0, half // step)
    def _(i):
        rows = pl.ds(pl.multiple_of(spot[1] * half + i * step, step), step)
        there = pl.ds(pl.multiple_of(i * step, step), step)
        lane = lax.broadcasted_iota(jnp.int32, (step, wide), 1)
        for way in range(2 * len(pairs)):
            slot = spot[0] ^ (2 * chips[way // 2] + way % 2)
            total = None
            for ref, (size, at) in zip(sources, places):
                part = window(ref, rows, slot * size, size, wide, at)
                total = part if total is None else total + part
            for index, gain in enumerate(gains):
                total = jnp.where(lane == extra_at + index, gain[rows, :].astype(jnp.float32), total)
            pairs[way // 2][way % 2, there, :] = total.astype(jnp.bfloat16)


def pack(weights, gains, spot, places, wide, chips, share):
    half = weights[0].shape[0] // share
    return pl.pallas_call(
        functools.partial(pack_kernel, places, len(gains), 16, chips),
        out_shape=(jax.ShapeDtypeStruct((2, half, wide), jnp.bfloat16),) * len(chips),
        in_specs=[SMEM] + [VMEM] * (len(weights) + len(gains)),
        out_specs=(VMEM,) * len(chips),
        compiler_params=pltpu.CompilerParams(vmem_limit_bytes=48 * 2**20),
        name="pack_weights",
    )(spot, *weights, *[gain[:, None] for gain in gains])


def assemble_kernel(shares, extra_at, spot, *refs):
    blocks, mates, whole = refs[: len(shares)], refs[len(shares)], refs[len(shares) + 1]
    rows = blocks[0].shape[1]
    passed = 0
    for (chip, share, other), block in zip(shares, blocks):
        part = rows // share
        for core in range(2):
            first = (spot[0] ^ (2 * chip + core)) * rows
            if share > 1:
                first = first + (spot[1] ^ other) * part
            at = pl.ds(pl.multiple_of(first, 16), part)
            whole[at, :] = mates[passed : passed + part, :] if core else block[0]
        passed += part
    if extra_at is not None:
        gains = refs[-1]
        first = extra_at // LANES * LANES
        for index in range(whole.shape[0] // LANES):
            at = pl.ds(index * LANES, LANES)
            part = whole[at, first : first + LANES].astype(jnp.float32).T
            gains[:, at] = pltpu.roll(part, LANES - extra_at % LANES, 0)[:8]


def assemble(pairs, shares, spot, extra_at):
    mates = swap_core(jnp.concatenate([pair[1] for pair in pairs], axis=0))
    rows, wide = pairs[0].shape[1:]
    shape = (2 * mates.shape[0], wide)
    out_shape = (jax.ShapeDtypeStruct(shape, jnp.bfloat16),)
    if extra_at is not None:
        out_shape += (jax.ShapeDtypeStruct((8, shape[0]), jnp.float32),)
    own = lambda pair: pl.BlockSpec((1,) + pair.shape[1:], lambda i: (0, 0, 0))
    full = lambda *shape: pl.BlockSpec(shape, lambda i: (0,) * len(shape))
    return pl.pallas_call(
        functools.partial(assemble_kernel, shares, extra_at),
        grid=(1,),
        out_shape=out_shape,
        in_specs=[SMEM] + [own(pair) for pair in pairs] + [full(*mates.shape)],
        out_specs=tuple(full(*o.shape) for o in out_shape),
        compiler_params=pltpu.CompilerParams(vmem_limit_bytes=56 * 2**20),
        name="assemble_weights",
    )(spot, *pairs, mates)


def after(values, *earlier):
    anywhere = pl.BlockSpec(memory_space=pl.ANY)
    return pl.pallas_call(
        lambda *refs: None,
        out_shape=tuple(jax.ShapeDtypeStruct(v.shape, v.dtype) for v in values),
        in_specs=[anywhere] * (len(values) + len(earlier)),
        out_specs=(anywhere,) * len(values),
        input_output_aliases={i: i for i in range(len(values))},
        name="after",
    )(*values, *earlier)


def product_kernel(first, index, x, y, *refs):
    out, total = refs[-2:]
    step = pl.program_id(0)

    @pl.when(step == 0)
    def _():
        total[...] = jnp.zeros_like(total)

    total[...] += lax.dot_general(
        x[:, first : first + total.shape[0]], y[...], (((0,), (0,)), ((), ())),
        preferred_element_type=jnp.float32,
    )

    @pl.when(step == pl.num_programs(0) - 1)
    def _():
        out[...] = total[: out.shape[0], :].astype(jnp.bfloat16)


def product(x, y, block, index, first, size, waits):
    rows, wide = y.shape
    step = rows // 4
    held = pad_lanes(size)
    return pl.pallas_call(
        functools.partial(product_kernel, first),
        grid_spec=pltpu.PrefetchScalarGridSpec(
            num_scalar_prefetch=1,
            grid=(4,),
            in_specs=[
                pl.BlockSpec((step, block), lambda k, at: (k, at[0])),
                pl.BlockSpec((step, wide), lambda k, at: (k, 0)),
            ]
            + [pl.BlockSpec(memory_space=pl.ANY)] * len(waits),
            out_specs=pl.BlockSpec((size, wide), lambda k, at: (0, 0)),
            scratch_shapes=[pltpu.VMEM((held, wide), jnp.float32)],
        ),
        out_shape=jax.ShapeDtypeStruct((size, wide), jnp.bfloat16),
        compiler_params=pltpu.CompilerParams(vmem_limit_bytes=48 * 2**20),
        cost_estimate=LITTLE,
        name="product",
    )(index, x, y, *waits)


def spread_kernel(places, count, me, *refs):
    blocks = refs[:count]
    weights = refs[count : count + len(places)]
    outs = refs[count + len(places) : count + 2 * len(places)]
    gain, held = refs[count + 2 * len(places) :]
    for way in range(count):
        held[me[0] ^ way] = blocks[way][...].astype(jnp.float32)
    for out in outs:
        out[...] = jnp.zeros_like(out)
    total = jnp.zeros(gain.shape, jnp.float32)
    for (size, at), weight, out in zip(places, weights, outs):
        full = out.shape[1]
        for index in range(count):
            start = index * size
            span = min(pad_lanes(size + start % LANES), full)
            aligned = min(start // LANES * LANES, full - span)
            shift = start - aligned
            low_lane = at // LANES * LANES
            width = pad_lanes(at - low_lane + size)
            values = held[index][:, low_lane : low_lane + width]
            lane = lax.broadcasted_iota(jnp.int32, values.shape, 1)
            inside = (lane >= at - low_lane) & (lane < at - low_lane + size)
            values = jnp.where(inside, values, 0.0)
            reach = max(span, width)
            if reach > width:
                filling = jnp.zeros((values.shape[0], reach - width), values.dtype)
                values = jnp.concatenate([values, filling], axis=1)
            turned = (shift - (at - low_lane)) % reach
            values = (pltpu.roll(values, turned, 1) if turned else values)[:, :span]
            out[:, aligned : aligned + span] += values
        product = out[...] * weight[...].astype(jnp.float32)
        total = total + jnp.sum(product, axis=1, keepdims=True)
    gain[...] = total


def spread(blocks, weights, me, places, step):
    count = len(blocks)
    rows, wide = weights[0].shape[0], blocks[0].shape[1]
    tile = lambda width: pl.BlockSpec((step, width), lambda i, at: (i, 0))
    block = pl.BlockSpec((step, wide), lambda i, at: (at[0] % 2 * (rows // step) + i, 0))
    return pl.pallas_call(
        functools.partial(spread_kernel, places, count),
        grid_spec=pltpu.PrefetchScalarGridSpec(
            num_scalar_prefetch=1,
            grid=(rows // step,),
            in_specs=[block] * count + [tile(w.shape[1]) for w in weights],
            out_specs=tuple(tile(w.shape[1]) for w in weights) + (tile(1),),
            scratch_shapes=[pltpu.VMEM((count, step, wide), jnp.float32)],
        ),
        out_shape=tuple(jax.ShapeDtypeStruct(w.shape, jnp.float32) for w in weights)
        + (jax.ShapeDtypeStruct((rows, 1), jnp.float32),),
        compiler_params=pltpu.CompilerParams(vmem_limit_bytes=56 * 2**20),
        name="spread_gradients",
    )(me[None].astype(jnp.int32), *blocks, *weights)


def wait(value, *earlier):
    return after((value,), *earlier)[0]


def mark_kernel(*refs):
    refs[-1][...] = jnp.zeros_like(refs[-1])


def flush(*earlier):
    token = pl.pallas_call(
        mark_kernel,
        out_shape=jax.ShapeDtypeStruct((16, LANES), jnp.bfloat16),
        in_specs=[pl.BlockSpec(memory_space=pl.ANY)] * len(earlier),
        out_specs=VMEM,
        name="mark",
    )(*earlier)
    return swap_core(token)


def normed(values):
    inverse = lax.rsqrt(jnp.mean(values * values, axis=-1, keepdims=True) + epsilon)
    return (values * inverse, inverse)


def norm_back(upward, unit_rows, inverse):
    return inverse * (upward - unit_rows * jnp.mean(upward * unit_rows, axis=-1, keepdims=True))


def layout(starts, slot_count):
    slot_index = lax.iota(jnp.int32, slot_count)
    segment_ids = lax.iota(jnp.int32, SEGS)
    segment_len = jnp.where(segment_ids == 0, TRUNK, TILE)
    inside = (slot_index[None, :] >= starts[:, None]) & (
        slot_index[None, :] < (starts + segment_len)[:, None]
    )
    return jnp.any(inside, axis=0)


def dot(left, right):
    return jnp.dot(left, right, preferred_element_type=jnp.float32)


def transpose_dot(left, right):
    return lax.dot_general(
        left, right, (((1,), (1,)), ((), ())), preferred_element_type=jnp.float32
    )


def rows_dot(left, right):
    return lax.dot_general(
        left, right, (((0,), (0,)), ((), ())), preferred_element_type=jnp.float32
    )


def low(values):
    return values.astype(jnp.bfloat16)


def plain(count):
    return count != 8 or lax.axis_size("replica") != 4


def gather_order(count):
    if plain(count):
        return [list(range(count))] * count
    ways = ((0, 1, 2, 3, 5, 4, 6, 7), (0, 1, 4, 5, 3, 2, 6, 7))
    return [[index ^ way for way in ways[index % 2]] for index in range(count)]


def swap_core(values):
    return lax.ppermute(values, "slot", [(i, i ^ 1) for i in range(8)])


def swap_near(values):
    return lax.ppermute(values, "slot", [(i, i ^ (4 if i % 2 else 2)) for i in range(8)])


def swap_far(values):
    return lax.ppermute(values, "slot", [(i, i ^ (2 if i % 2 else 4)) for i in range(8)])


def gather(own):
    count = lax.axis_size("slot")
    if plain(count):
        return jnp.split(lax.all_gather(own, "slot", axis=0, tiled=True), 4, axis=0)
    block = own.shape[0]
    chip = jnp.concatenate([own, swap_core(own)], axis=0)
    near = swap_near(chip)
    corner = swap_far(near[:block])
    return [chip, near, swap_core(near), jnp.concatenate([corner, swap_core(corner)], axis=0)]


def scatter(parts, *between):
    count = lax.axis_size("slot")
    if plain(count):
        whole = jnp.concatenate(parts, axis=0)
        return lax.psum_scatter(whole, "slot", scatter_dimension=0, tiled=True).astype(
            jnp.float32
        )
    chip, near, side, corner = parts
    block = chip.shape[0] // 2
    wide = lambda values: values.astype(jnp.float32)
    near_sum = low(wide(near) + wide(swap_core(side)))
    corner_sum = low(wide(corner[:block]) + wide(swap_core(corner[block:])))
    arrived = swap_far(corner_sum), swap_near(near_sum[block:])
    if between:
        arrived = after(arrived, *between[0](corner_sum))
    near_own = low(wide(near_sum[:block]) + wide(arrived[0]))
    other = low(wide(chip[block:]) + wide(arrived[1]))
    arrived = swap_near(near_own), swap_core(other)
    if between:
        arrived = after(arrived, *between[1](near_own))
    return wide(chip[:block]) + wide(arrived[0]) + wide(arrived[1])


def send(block, way):
    count = lax.axis_size("slot")
    if way == 0:
        return block
    return lax.ppermute(block, "slot", [(i, i ^ way) for i in range(count)])


def sum_trees(part):
    return lax.psum(part, "replica")


def plain_columns(weights, gains, places, wide, heads_in):
    count = lax.axis_size("slot")
    extra_at = sum(size for size, _ in places)
    blocks = jnp.zeros((count, weights[0].shape[0], wide), jnp.bfloat16)
    for weight, (size, at), heads in zip(weights, places, heads_in):
        blocks = blocks.at[:, :, at : at + size].set(split_columns(weight, count, heads))
    for index, gain in enumerate(gains):
        blocks = blocks.at[:, :, extra_at + index].set(gain[None])
    whole = lax.all_to_all(blocks, "slot", 0, 0).reshape(-1, wide)
    return whole, whole[:, extra_at : extra_at + len(gains)].T.astype(jnp.float32)


def send_pairs(pairs):
    return [send(pair, 2 * chip) for chip, pair in enumerate(pairs)]


def swap_halves(pairs):
    trees = lax.axis_size("replica")
    return lax.ppermute(pairs, "replica", [(i, i ^ 1) for i in range(trees)])


def plain_rows(gradient, weights, places, heads_in):
    count = lax.axis_size("slot")
    rows = gradient.shape[0] // count
    blocks = lax.all_to_all(gradient.reshape(count, rows, -1), "slot", 0, 0)
    blocks = sum_trees(blocks).astype(jnp.float32)
    parts = [
        join_columns(blocks[:, :, at : at + size], heads)
        for (size, at), heads in zip(places, heads_in)
    ]
    products = [jnp.sum(p * w.astype(jnp.float32), axis=1) for p, w in zip(parts, weights)]
    return parts, sum(products)


def split_columns(weight, count, heads_in=None):
    rows, columns = weight.shape
    if heads_in is not None and heads_in < count:
        weight = weight.reshape(rows, heads_in, columns // heads_in)
        weight = jnp.repeat(weight, count // heads_in, axis=1)
    else:
        weight = weight.reshape(rows, count, columns // count)
    return weight.transpose(1, 0, 2)


def join_columns(blocks, heads_in=None):
    count, rows, columns = blocks.shape
    if heads_in is not None and heads_in < count:
        blocks = jnp.sum(blocks.reshape(heads_in, count // heads_in, rows, columns), axis=1)
        count = heads_in
    return blocks.transpose(1, 0, 2).reshape(rows, count * columns)


def shards(
    layer_in,
    seg_starts,
    seg_parents,
    w_query,
    w_key,
    w_value,
    w_out,
    w_gate,
    w_up,
    w_down,
    gain_attn,
    gain_ffn,
    out_cotangent,
):
    count = lax.axis_size("slot")
    me = lax.axis_index("slot")
    row_count = layer_in.shape[1]
    slot_count = row_count * count
    features = layer_in.shape[2]
    kv_heads = w_key.shape[1] // HEAD_DIM
    q_width = w_query.shape[1] // count
    heads_width = q_width + 2 * HEAD_DIM
    heads_wide = pad_lanes(heads_width + 2)
    hidden = w_down.shape[0]
    hidden_wide = pad_lanes(hidden)
    starts, parents = seg_starts[0], seg_parents[0]
    tile_starts = jnp.concatenate([lax.iota(jnp.int32, TRUNK_TILES) * TILE, starts[1:]])
    order = jnp.asarray(gather_order(count), jnp.int32)[me]
    tables = turn_tables()
    live = layout(starts, slot_count).astype(jnp.float32).reshape(count, row_count)
    my_live = live[me]

    def cut(values):
        return jnp.split(values, 4, axis=0)

    def blocks_of(parts):
        return jnp.concatenate(parts, axis=0).reshape(count, row_count, parts[0].shape[-1])

    special = not plain(count)
    head_weights = (w_query, w_key, w_value)
    head_places = ((q_width, 0), (HEAD_DIM, q_width), (HEAD_DIM, q_width + HEAD_DIM))
    head_counts = (None, kv_heads, kv_heads)
    hidden_places = ((hidden, 0), (hidden, hidden_wide))
    gain_pair = (gain_attn, gain_ffn)

    def attn_part(part):
        return low(normed(part.astype(jnp.float32))[0] * full_gain_attn)

    if special:
        flat = jnp.stack([me, jnp.zeros_like(me)]).astype(jnp.int32)
        chip = jnp.concatenate([layer_in[0], swap_core(layer_in[0])], axis=0)
        near = swap_near(chip)
        spot = jnp.stack([me, lax.axis_index("replica") % 2]).astype(jnp.int32)
        chips = (0, 1, 2, 3)
        packed = pack(head_weights, gain_pair, flat, head_places, heads_wide, chips, 1)
        hidden_weights = (w_gate, w_up)
        hidden_packed = pack(hidden_weights, (), flat, hidden_places, 2 * hidden_wide, chips[:3], 1)
        hidden_packed += pack(hidden_weights, (), spot, hidden_places, 2 * hidden_wide, chips[3:], 2)
        head_pairs = send_pairs(packed)
        head_pairs = after(head_pairs, flush(hidden_packed[0]))
        whole_shares = tuple((chip, 1, 0) for chip in chips)
        w_heads, gains = assemble(head_pairs, whole_shares, flat, heads_width)
        full_gain_attn, full_gain_ffn = gains[0], gains[1]
        near = wait(near, head_pairs[1])
        corner, side = swap_far(near[:row_count]), swap_core(near)
        hidden_pairs = send_pairs(after(hidden_packed, near))
        token = flush(near)
        attn_parts = [attn_part(part) for part in (wait(chip, token), near, side)]
        parts = [dot(part, w_heads) for part in attn_parts]
        corner = jnp.concatenate([corner, swap_core(corner)], axis=0)
        attn_parts.append(attn_part(corner))
        parts.append(dot(attn_parts[3], w_heads))
        qkv = blocks_of(parts)
    else:
        layer_parts = gather(layer_in[0])
        w_heads, gains = plain_columns(
            head_weights, gain_pair, head_places, heads_wide, head_counts
        )
        w_hidden, _ = plain_columns(
            (w_gate, w_up), (), hidden_places, 2 * hidden_wide, (None, None)
        )
        full_gain_attn, full_gain_ffn = gains[0], gains[1]
        attn_parts = [attn_part(part) for part in layer_parts]
        qkv = blocks_of([dot(part, w_heads) for part in attn_parts])
    attended, *kept = attend_forward(q_width // HEAD_DIM, qkv, tables, tile_starts, parents, order)
    attended = attended.reshape(slot_count, q_width)
    if special:
        hidden_pairs = after(hidden_pairs, attended)
        hidden_pairs += (swap_halves(hidden_pairs[3]),)
        attended = wait(attended, hidden_pairs[3])
    residual = layer_in[0].astype(jnp.float32)
    middle = residual + scatter([low(dot(part, w_out)) for part in cut(attended)])

    w_lower = jnp.pad(w_down, ((0, hidden_wide - hidden), (0, 0)))
    live_rows = jnp.broadcast_to(live.reshape(slot_count, 1), (slot_count, LANES))
    unit_ffn, rms_ffn = normed(middle)
    ffn_input = low(unit_ffn * full_gain_ffn)
    if special:
        feed = lambda index, part, down, held: dense(
            index, order, part, down, live_rows, w_hidden, w_lower, held
        )
        hidden_shares = whole_shares[:3] + ((3, 2, 0), (3, 2, 1))
        (w_hidden,) = assemble(hidden_pairs, hidden_shares, spot, None)
        cotangent = wait(out_cotangent[0], attended)
        chip_down = jnp.concatenate([cotangent, swap_core(cotangent)], axis=0)
        near_down = swap_near(chip_down)
        chip_part = jnp.concatenate([ffn_input, swap_core(ffn_input)], axis=0)
        near_part = swap_near(chip_part)
        chip_back, chip_out, held = feed(0, chip_part, chip_down, ())
        near_down = wait(near_down, chip_back)
        near_part = wait(near_part, near_down)
        corner, corner_down = swap_far(near_part[:row_count]), swap_far(near_down[:row_count])
        side_part, side_down = swap_core(near_part), swap_core(near_down)
        near_back, near_out, held = feed(1, near_part, near_down, held)
        side_back, side_out, held = feed(2, side_part, side_down, held)
        corner, corner_down = after((corner, corner_down), near_back)
        corner_part = jnp.concatenate([corner, swap_core(corner)], axis=0)
        corner_down = jnp.concatenate([corner_down, swap_core(corner_down)], axis=0)
        corner_back, corner_out, held = feed(3, corner_part, corner_down, held)
        back_parts = [chip_back, near_back, side_back, corner_back]
        out_parts = [chip_out, near_out, side_out, corner_out]
    else:
        held, back_parts, out_parts = (), [], []
        pairs = zip(gather(ffn_input), gather(out_cotangent[0]))
        for index, (part, down) in enumerate(pairs):
            back, out, held = dense(
                index, lax.iota(jnp.int32, 4), part, down, live_rows, w_hidden, w_lower, held
            )
            back_parts.append(back)
            out_parts.append(out)
    ffn_rows, down_rows, active_rows, hidden_rows = held
    upstream = out_cotangent[0].astype(jnp.float32) * my_live[:, None]

    def middle_of(ffn_input_grad):
        return upstream + norm_back(ffn_input_grad * full_gain_ffn, unit_ffn, rms_ffn)

    def hidden_part(chip, *waits):
        span = 2 * features // count
        index = ((me ^ chip) // 2)[None].astype(jnp.int32)
        return product(ffn_rows, hidden_rows, span, index, 0, span, waits)

    def to_heads(part):
        return low(transpose_dot(part, w_out))

    def proj_part():
        return low(sum(rows_dot(a, b) for a, b in zip(cut(attended), branch_parts)))

    def heads_part():
        return low(sum(rows_dot(a, b) for a, b in zip(attn_parts, head_parts)))

    if special:
        hidden_parts = []

        def all_hidden(mark):
            for chip in (0, 2, 4, 6):
                hidden_parts.append(hidden_part(chip, mark, *hidden_parts[-1:]))
            return hidden_parts[-1:]

        ffn_input_grad = scatter(back_parts, all_hidden, lambda mark: (mark,))
        middle_grad = middle_of(ffn_input_grad)
        branch = low(middle_grad)
        chip_part = jnp.concatenate([branch, swap_core(branch)], axis=0)
        near_part = swap_near(chip_part)
        hidden_sums = lax.psum(tuple(hidden_parts), "replica")
        side_part = swap_core(near_part)
        corner = swap_far(near_part[:row_count])
        index = jnp.zeros((1,), jnp.int32)
        grad_down = product(active_rows, down_rows, hidden_wide, index, 0, hidden, (chip_part,))
        corner = wait(corner, grad_down)
        corner_part = jnp.concatenate([corner, swap_core(corner)], axis=0)
        branch_parts = [chip_part, near_part, side_part, corner_part]
    else:
        middle_grad = middle_of(scatter(back_parts))
        branch_parts = gather(low(middle_grad))
    attended_grad = blocks_of([to_heads(part) for part in branch_parts])
    head_grads = attend_backward(attended_grad, kept, tables, tile_starts, parents, order)
    head_parts = cut(head_grads.reshape(slot_count, heads_wide))
    input_parts = [low(transpose_dot(part, w_heads)) for part in head_parts]
    attn_input_grad = scatter(input_parts)
    unit_attn, rms_attn = normed(residual)
    grad_in = low(
        middle_grad + norm_back(attn_input_grad * full_gain_attn, unit_attn, rms_attn)
    )
    grad_proj, grad_heads = proj_part(), heads_part()
    if special:
        out_parts = after(out_parts, grad_in)
    layer_out = low(middle + scatter(out_parts))

    if special:

        def settled(sums):
            blocks = []
            for chip, summed in zip(range(0, count, 2), sums):
                block = send(summed, chip)
                blocks += [block, swap_core(block)]
            return blocks

        hidden_sums = after(hidden_sums, grad_in, grad_heads, grad_proj)
        grad_heads, grad_proj = after((grad_heads, grad_proj), *hidden_sums)
        grad_heads, grad_proj = lax.psum((grad_heads, grad_proj), "replica")
        blocks = settled(hidden_sums)
        grad_gate, grad_up, gain_ffn_sum = spread(blocks, (w_gate, w_up), me, hidden_places, 32)
        grad_heads, grad_proj = after((grad_heads, grad_proj), grad_gate)
        grad_down = lax.psum(wait(grad_down, grad_heads), "replica")
        span = 2 * features // count
        blocks = settled(
            [
                lax.dynamic_slice_in_dim(grad_heads, (me ^ chip) // 2 * span, span)
                for chip in range(0, count, 2)
            ]
        )
        grad_query, grad_key, grad_value, gain_attn_sum = spread(
            blocks, head_weights, me, head_places, 64
        )
        gain_ffn_sum, gain_attn_sum = gain_ffn_sum[:, 0], gain_attn_sum[:, 0]
        grad_down = wait(grad_down, grad_query)
    else:
        grad_down = sum_trees(low(rows_dot(active_rows, down_rows)[:hidden]))
        (grad_gate, grad_up), gain_ffn_sum = plain_rows(
            low(rows_dot(ffn_rows, hidden_rows)), (w_gate, w_up), hidden_places, (None, None)
        )
        grad_proj = sum_trees(grad_proj)
        (grad_query, grad_key, grad_value), gain_attn_sum = plain_rows(
            grad_heads, head_weights, head_places, head_counts
        )
    return (
        layer_out[None],
        grad_in[None],
        grad_query,
        grad_key,
        grad_value,
        grad_proj.astype(jnp.float32),
        grad_gate,
        grad_up,
        grad_down.astype(jnp.float32),
        gain_attn_sum / gain_attn.astype(jnp.float32),
        gain_ffn_sum / gain_ffn.astype(jnp.float32),
    )


def solution(mesh):
    tokens, tree, rows, vector = P("replica", "slot", None), P("replica", None), P("slot", None), P("slot")
    in_specs = (tokens, tree, tree) + (rows,) * 7 + (vector, vector, tokens)
    out_specs = (tokens, tokens) + (rows,) * 7 + (vector, vector)
    return jax.shard_map(shards, mesh=mesh, in_specs=in_specs, out_specs=out_specs, check_vma=False)
```

```python
import functools
import jax
import jax.numpy as jnp
from jax import lax
from jax.experimental import pallas as pl
from jax.experimental.pallas import tpu as pltpu
from jax.sharding import PartitionSpec as P

HEAD_DIM = 80
TRUNK = 768
SEGS = 13
TILE = 128
NBRANCH = 4
SEG_TILES = TRUNK // TILE + SEGS - 1
TRUNK_TILES = TRUNK // TILE
LANES = 128
BLOCK = 256
epsilon = 1e-05
masked_score = -1e30
rope_theta = 10000.0
log2e = 1.4426950408889634


def pad_lanes(width):
    return -(-width // LANES) * LANES


def turn_tables():
    half = HEAD_DIM // 2
    frequency = jnp.power(rope_theta, -2.0 * lax.iota(jnp.float32, half) / HEAD_DIM)
    angle = lax.iota(jnp.float32, TRUNK + 2 * TILE)[:, None] * frequency[None, :]
    cosine, sine = jnp.cos(angle), jnp.sin(angle)
    none = jnp.zeros_like(sine)
    tail = jnp.zeros((angle.shape[0], LANES - HEAD_DIM), jnp.float32)
    return jnp.stack(
        [
            jnp.concatenate([cosine, cosine, tail], axis=1),
            jnp.concatenate([none, sine, tail], axis=1),
            jnp.concatenate([-sine, none, tail], axis=1),
        ]
    )


def tile_base(tile):
    return jnp.where(
        tile < TRUNK_TILES,
        tile * TILE,
        jnp.where(tile < TRUNK_TILES + NBRANCH, TRUNK, TRUNK + TILE),
    )


def take_head(rows, head):
    width = rows.shape[1]
    shift = (width - head * HEAD_DIM) % width
    return (pltpu.roll(rows, shift, 1) if shift else rows)[:, :LANES]


def put_head(part, head, width):
    wide = jnp.concatenate(
        [part, jnp.zeros((part.shape[0], width - LANES), part.dtype)], axis=1
    )
    return pltpu.roll(wide, head * HEAD_DIM, 1) if head else wide


def turn(rows, tables, sign):
    half = HEAD_DIM // 2
    cosine, up, down = tables
    swapped = pltpu.roll(rows, half, 1) * up + pltpu.roll(rows, LANES - half, 1) * down
    return rows * cosine + swapped if sign > 0 else rows * cosine - swapped


def head_lanes(rows):
    lane = lax.broadcasted_iota(jnp.int32, rows.shape, 1)
    return jnp.where(lane < HEAD_DIM, rows, 0.0)


def read_rows(ref, start):
    aligned = pl.multiple_of(start // 8 * 8, 8)
    rows = ref[pl.ds(aligned, TILE + 8), :]
    return pltpu.roll(rows, (TILE + 8) - (start - aligned), 0)[:TILE]


def write_rows(ref, start, rows):
    aligned = pl.multiple_of(start // 8 * 8, 8)
    offset = start - aligned
    at = pl.ds(aligned, TILE + 8)
    wide = jnp.concatenate([rows, jnp.zeros((8, rows.shape[1]), rows.dtype)], axis=0)
    wide = pltpu.roll(wide, offset, 0)
    index = lax.broadcasted_iota(jnp.int32, wide.shape, 0)
    inside = (index >= offset) & (index < offset + TILE)
    ref[at, :] = jnp.where(inside, wide, ref[at, :])


def nt(a, b):
    return lax.dot_general(a, b, (((1,), (1,)), ((), ())), preferred_element_type=jnp.float32)


def nn(a, b):
    return lax.dot_general(a, b, (((1,), (0,)), ((), ())), preferred_element_type=jnp.float32)


def causal(columns):
    key = lax.broadcasted_iota(jnp.int32, (TILE, columns), 0)
    query = lax.broadcasted_iota(jnp.int32, (TILE, columns), 1) % TILE
    return key <= query


def each_tile(tile_fn, parent_of):
    for tile in range(TRUNK_TILES):
        tile_fn(tile, tile * TILE, None)

    @pl.loop(TRUNK_TILES, TRUNK_TILES + NBRANCH)
    def _(tile):
        tile_fn(tile, TRUNK, None)

    @pl.loop(TRUNK_TILES + NBRANCH, SEG_TILES)
    def _(tile):
        tile_fn(tile, TRUNK, parent_of(tile) + TRUNK_TILES - 1)


def tile_rows(tile, size=TILE):
    if isinstance(tile, int):
        return pl.ds(tile * size, size)
    return pl.ds(pl.multiple_of(tile * size, size), size)


def forward_kernel(
    group, starts, parents, order, qkv, tables,
    attended, q_keep, k_keep, v_keep, lse_keep,
    slots, v_turned, out_rows,
):
    slot_count = qkv.shape[0] * qkv.shape[1]
    width = slots.shape[1]
    out_width = out_rows.shape[1]
    block = qkv.shape[1]

    @pl.loop(0, qkv.shape[0])
    def _(i):
        slots[pl.ds(pl.multiple_of(order[i] * block, 8), block), :] = qkv[i]

    @pl.loop(0, slot_count // TILE)
    def _(i):
        rows = tile_rows(i)
        own = take_head(slots[rows, :], group + 1)
        own = head_lanes(own).astype(jnp.bfloat16).astype(jnp.float32)
        total = put_head(own, 0, out_width)
        for head in range(1, group):
            total = total + put_head(own, head, out_width)
        out_rows[rows, :] = total

    @pl.loop(0, SEG_TILES)
    def _(tile):
        rows = read_rows(slots, starts[tile])
        base = pl.ds(pl.multiple_of(tile_base(tile), TILE), TILE)
        turns = tuple(tables[t, base, :] for t in range(3))
        for head in range(group):
            turned = turn(take_head(rows, head), turns, 1) * (HEAD_DIM**-0.5 * log2e)
            at = pl.ds(pl.multiple_of(tile * (group * TILE) + head * TILE, TILE), TILE)
            q_keep[at, :] = turned.astype(jnp.bfloat16)
        k_keep[tile_rows(tile), :] = turn(take_head(rows, group), turns, 1).astype(jnp.bfloat16)
        own = head_lanes(take_head(rows, group + 1))
        v_keep[tile_rows(tile), :] = own.astype(jnp.bfloat16)
        v_turned[:, tile_rows(tile)] = own.T.astype(jnp.bfloat16)

    columns = group * TILE

    def attend(tile, full, parent):
        queries = q_keep[tile_rows(tile, columns), :]
        keys = [pl.ds(0, full)] if full else []
        if parent is not None:
            keys.append(tile_rows(parent))
        keys.append(tile_rows(tile))
        scores = [nt(k_keep[at, :], queries) for at in keys]
        scores[-1] = jnp.where(causal(columns), scores[-1], masked_score)
        top = functools.reduce(jnp.maximum, [jnp.max(s, axis=0, keepdims=True) for s in scores])
        weights = [jnp.exp2(s - top) for s in scores]
        total = functools.reduce(jnp.add, [jnp.sum(w, axis=0, keepdims=True) for w in weights])
        mixed = functools.reduce(
            jnp.add,
            [nn(v_turned[:, at], w.astype(jnp.bfloat16)) for at, w in zip(keys, weights)],
        )
        mixed = mixed * (1.0 / total)
        lse_keep[pl.ds(tile, 1)] = (top + jnp.log2(total))[None]
        result = put_head(mixed[:, :TILE].T, 0, out_width)
        for head in range(1, group):
            result = result + put_head(
                mixed[:, head * TILE : (head + 1) * TILE].T, head, out_width
            )
        write_rows(out_rows, starts[tile], result)

    each_tile(attend, lambda tile: parents[tile - TRUNK_TILES + 1])

    kept = attended.shape[-1]

    @pl.loop(0, qkv.shape[0])
    def _(i):
        rows = out_rows[pl.ds(pl.multiple_of(order[i] * block, 8), block), :]
        attended[i] = rows[:, :kept].astype(jnp.bfloat16)


def backward_kernel(
    group, starts, parents, order, attended_grad, q_keep, k_keep, v_keep, lse_keep, tables,
    grads,
    slots, do_keep, k_turned, dk, dv, dq, out_rows,
):
    slot_count = attended_grad.shape[0] * attended_grad.shape[1]
    in_width = slots.shape[1]
    width = out_rows.shape[1]
    block = attended_grad.shape[1]
    kept = attended_grad.shape[2]
    columns = group * TILE

    slots[...] = jnp.zeros_like(slots)

    @pl.loop(0, attended_grad.shape[0])
    def _(i):
        at = pl.ds(pl.multiple_of(order[i] * block, 8), block)
        slots[at, :kept] = attended_grad[i].astype(jnp.float32)

    @pl.loop(0, slot_count // TILE)
    def _(i):
        rows = slots[tile_rows(i), :]
        total = take_head(rows, 0)
        for head in range(1, group):
            total = total + take_head(rows, head)
        out_rows[tile_rows(i), :] = put_head(head_lanes(total), group + 1, width)

    @pl.loop(0, SEG_TILES)
    def _(tile):
        rows = read_rows(slots, starts[tile])
        for head in range(group):
            at = pl.ds(pl.multiple_of(tile * columns + head * TILE, TILE), TILE)
            do_keep[at, :] = head_lanes(take_head(rows, head)).astype(jnp.bfloat16)
        k_turned[:, tile_rows(tile)] = (
            k_keep[tile_rows(tile), :].astype(jnp.float32).T.astype(jnp.bfloat16)
        )

    dk[...] = jnp.zeros_like(dk)
    dv[...] = jnp.zeros_like(dv)

    def attend(tile, full, parent):
        queries = q_keep[tile_rows(tile, columns), :]
        upward = do_keep[tile_rows(tile, columns), :]
        lse = lse_keep[pl.ds(tile, 1)][0]
        keys = [pl.ds(0, full)] if full else []
        if parent is not None:
            keys.append(tile_rows(parent))
        keys.append(tile_rows(tile))
        probs = [jnp.exp2(nt(k_keep[at, :], queries) - lse) for at in keys]
        probs[-1] = jnp.where(causal(columns), probs[-1], 0.0)
        prob_grads = [nt(v_keep[at, :], upward) for at in keys]
        row_dot = functools.reduce(
            jnp.add,
            [jnp.sum(p * g, axis=0, keepdims=True) for p, g in zip(probs, prob_grads)],
        )
        mixed = None
        for at, p, g in zip(keys, probs, prob_grads):
            score_grad = (p * (g - row_dot)).astype(jnp.bfloat16)
            dv[at, :] += nn(p.astype(jnp.bfloat16), upward)
            dk[at, :] += nn(score_grad, queries)
            part = nn(k_turned[:, at], score_grad)
            mixed = part if mixed is None else mixed + part
        base = pl.ds(pl.multiple_of(tile_base(tile), TILE), TILE)
        turns = tuple(tables[t, base, :] for t in range(3))
        result = None
        for head in range(group):
            part = turn(mixed[:, head * TILE : (head + 1) * TILE].T, turns, -1) * HEAD_DIM**-0.5
            part = put_head(part, head, width)
            result = part if result is None else result + part
        dq[tile_rows(tile), :] = result

    each_tile(attend, lambda tile: parents[tile - TRUNK_TILES + 1])

    @pl.loop(0, SEG_TILES)
    def _(tile):
        rows = tile_rows(tile)
        base = pl.ds(pl.multiple_of(tile_base(tile), TILE), TILE)
        turns = tuple(tables[t, base, :] for t in range(3))
        key_part = turn(dk[rows, :], turns, -1) * (1.0 / log2e)
        total = dq[rows, :] + put_head(key_part, group, width)
        total = total + put_head(dv[rows, :], group + 1, width)
        write_rows(out_rows, starts[tile], total)

    @pl.loop(0, attended_grad.shape[0])
    def _(i):
        rows = out_rows[pl.ds(pl.multiple_of(order[i] * block, 8), block), :]
        grads[i] = rows[:, : grads.shape[2]].astype(jnp.bfloat16)


def dense_kernel(
    chunk, held, order, x_far, down_far, live_far, w_far, lower_far, *refs
):
    refs = refs[held:]
    whole, out_far, back_far, refs = refs[:4], refs[4], refs[5], refs[6:]
    x, down, live, w, lower, both, upward, active, masked, hidden, back, out, sems = refs
    wide = lower.shape[0]
    blocks = order.shape[0] // 4
    block = x.shape[0] // blocks
    inside = [pl.ds(i * block, block) for i in range(blocks)]
    rows = [
        pl.ds(pl.multiple_of(order[chunk * blocks + i] * block, 16), block) for i in range(blocks)
    ]

    def copies(near, far, first, inward):
        ends = [(near.at[a], far.at[b]) for a, b in zip(inside, rows)]
        return [
            pltpu.make_async_copy(*(reversed(pair) if inward else pair), sems.at[first + i])
            for i, pair in enumerate(ends)
        ]

    arrivals = copies(live, live_far, 0, True)
    arrivals.append(pltpu.make_async_copy(down_far, down, sems.at[2]))
    arrivals.append(pltpu.make_async_copy(lower_far, lower, sems.at[3]))
    later = [pltpu.make_async_copy(x_far, x, sems.at[4]), pltpu.make_async_copy(w_far, w, sems.at[5])]
    for copy in arrivals + later:
        copy.start()
    for copy in arrivals:
        copy.wait()
    upward[...] = nt(down[...], lower[...])
    for copy in later:
        copy.wait()

    @pl.loop(0, 2 * wide // BLOCK)
    def _(t):
        at = tile_rows(t, BLOCK)
        both[:, at] = nn(x[...], w[:, at])

    @pl.loop(0, x.shape[0] // 32)
    def _(i):
        at = tile_rows(i, 32)
        gate, up = both[at, :wide], both[at, wide:]
        alive = live[at, :1]
        grad = upward[at, :] * alive
        sigmoid = 1.0 / (1.0 + jnp.exp(-gate))
        silu = gate * sigmoid
        active_now = silu * up
        active[at, :] = active_now.astype(jnp.bfloat16)
        masked[at, :] = (active_now * alive).astype(jnp.bfloat16)
        gate_grad = grad * up * sigmoid * (1.0 + gate * (1.0 - sigmoid))
        hidden[at, :wide] = gate_grad.astype(jnp.bfloat16)
        hidden[at, wide:] = (grad * silu).astype(jnp.bfloat16)

    leaving = []
    for index, near in enumerate((x, down, masked, hidden)):
        leaving += copies(near, whole[index], 6 + 2 * index, False)
    for copy in leaving:
        copy.start()
    half = x.shape[1] // 2
    for first in (0, half):
        at = pl.ds(first, half)
        back[:, at] = nt(hidden[...], w[at, :]).astype(jnp.bfloat16)
    last = [pltpu.make_async_copy(back, back_far, sems.at[14])]
    last[0].start()
    for first in (0, half):
        at = pl.ds(first, half)
        out[:, at] = nn(active[...], lower[:, at]).astype(jnp.bfloat16)
    last.append(pltpu.make_async_copy(out, out_far, sems.at[15]))
    last[1].start()
    for copy in leaving + last:
        copy.wait()


def dense(chunk, order, x, down, live, w, lower, held):
    rows, features = x.shape
    wide = lower.shape[0]
    slots = 4 * rows
    low_of = lambda *shape: jax.ShapeDtypeStruct(shape, jnp.bfloat16)
    far = pl.BlockSpec(memory_space=pl.ANY)
    keep = lambda *shape: pltpu.VMEM(shape, jnp.bfloat16)
    aliases = {6 + i: i for i in range(len(held))}
    results = pl.pallas_call(
        functools.partial(dense_kernel, chunk, len(held)),
        out_shape=(
            low_of(slots, features), low_of(slots, features), low_of(slots, wide),
            low_of(slots, 2 * wide), low_of(rows, features), low_of(rows, features),
        ),
        in_specs=[SMEM] + [far] * (5 + len(held)),
        out_specs=(far,) * 6,
        scratch_shapes=[
            keep(rows, features), keep(rows, features), pltpu.VMEM((rows, LANES), jnp.float32),
            keep(features, 2 * wide), keep(wide, features),
            pltpu.VMEM((rows, 2 * wide), jnp.float32), pltpu.VMEM((rows, wide), jnp.float32),
            keep(rows, wide), keep(rows, wide), keep(rows, 2 * wide),
            keep(rows, features), keep(rows, features),
            pltpu.SemaphoreType.DMA((16,)),
        ],
        input_output_aliases=aliases,
        compiler_params=pltpu.CompilerParams(vmem_limit_bytes=60 * 2**20),
        name="dense",
    )(order, x, down, live, w, lower, *held)
    return results[5], results[4], results[:4]


LITTLE = pl.CostEstimate(flops=1, bytes_accessed=1, transcendentals=0)
SMEM = pl.BlockSpec(memory_space=pltpu.SMEM)
VMEM = pl.BlockSpec(memory_space=pltpu.VMEM)


def attend_forward(group, qkv, tables, starts, parents, order):
    blocks, block, width = qkv.shape
    slot_count = blocks * block
    wide = pad_lanes(width)
    out_wide = pad_lanes(group * HEAD_DIM)
    live = SEG_TILES * TILE
    return pl.pallas_call(
        functools.partial(forward_kernel, group),
        out_shape=(
            jax.ShapeDtypeStruct((blocks, block, group * HEAD_DIM), jnp.bfloat16),
            jax.ShapeDtypeStruct((group * live, LANES), jnp.bfloat16),
            jax.ShapeDtypeStruct((live, LANES), jnp.bfloat16),
            jax.ShapeDtypeStruct((live, LANES), jnp.bfloat16),
            jax.ShapeDtypeStruct((SEG_TILES, 1, group * TILE), jnp.float32),
        ),
        in_specs=[SMEM, SMEM, SMEM, VMEM, VMEM],
        out_specs=(VMEM,) * 5,
        scratch_shapes=[
            pltpu.VMEM((slot_count + 8, wide), jnp.float32),
            pltpu.VMEM((LANES, live), jnp.bfloat16),
            pltpu.VMEM((slot_count + 8, out_wide), jnp.float32),
        ],
        compiler_params=pltpu.CompilerParams(vmem_limit_bytes=48 * 2**20),
        name="tree_forward",
    )(starts, parents, order, qkv, tables)


def attend_backward(attended_grad, kept, tables, starts, parents, order):
    blocks, block, width = attended_grad.shape
    slot_count = blocks * block
    group = width // HEAD_DIM
    wide = pad_lanes((group + 2) * HEAD_DIM + 2)
    in_wide = pad_lanes(width)
    live = SEG_TILES * TILE
    return pl.pallas_call(
        functools.partial(backward_kernel, group),
        out_shape=jax.ShapeDtypeStruct((blocks, block, wide), jnp.bfloat16),
        in_specs=[SMEM, SMEM, SMEM] + [VMEM] * 6,
        out_specs=VMEM,
        scratch_shapes=[
            pltpu.VMEM((slot_count + 8, in_wide), jnp.float32),
            pltpu.VMEM((group * live, LANES), jnp.bfloat16),
            pltpu.VMEM((LANES, live), jnp.bfloat16),
            pltpu.VMEM((live, LANES), jnp.float32),
            pltpu.VMEM((live, LANES), jnp.float32),
            pltpu.VMEM((live, wide), jnp.float32),
            pltpu.VMEM((slot_count + 8, wide), jnp.float32),
        ],
        compiler_params=pltpu.CompilerParams(vmem_limit_bytes=56 * 2**20),
        cost_estimate=LITTLE,
        name="tree_backward",
    )(starts, parents, order, attended_grad, *kept, tables)


def window(ref, rows, start, size, wide, at):
    full = ref.shape[-1]
    span = min(pad_lanes(size + LANES - 1), full)
    aligned = jnp.minimum(start // LANES * LANES, full - span)
    shift = start - aligned
    values = ref[rows, pl.ds(pl.multiple_of(aligned, LANES), span)].astype(jnp.float32)
    lane = lax.broadcasted_iota(jnp.int32, values.shape, 1)
    values = jnp.where((lane >= shift) & (lane < shift + size), values, 0.0)
    reach = max(span, wide)
    if reach > span:
        filling = jnp.zeros((values.shape[0], reach - span), values.dtype)
        values = jnp.concatenate([values, filling], axis=1)
    return pltpu.roll(values, lax.rem(at - shift + reach, reach), 1)[:, :wide]


def pack_kernel(places, extras, step, chips, spot, *refs):
    sources, gains = refs[: len(places)], refs[len(places) : len(places) + extras]
    pairs = refs[len(places) + extras :]
    half, wide = pairs[0].shape[1:]
    extra_at = sum(size for size, _ in places)

    @pl.loop(0, half // step)
    def _(i):
        rows = pl.ds(pl.multiple_of(spot[1] * half + i * step, step), step)
        there = pl.ds(pl.multiple_of(i * step, step), step)
        lane = lax.broadcasted_iota(jnp.int32, (step, wide), 1)
        for way in range(2 * len(pairs)):
            slot = spot[0] ^ (2 * chips[way // 2] + way % 2)
            total = None
            for ref, (size, at) in zip(sources, places):
                part = window(ref, rows, slot * size, size, wide, at)
                total = part if total is None else total + part
            for index, gain in enumerate(gains):
                total = jnp.where(lane == extra_at + index, gain[rows, :].astype(jnp.float32), total)
            pairs[way // 2][way % 2, there, :] = total.astype(jnp.bfloat16)


def pack(weights, gains, spot, places, wide, chips, share):
    half = weights[0].shape[0] // share
    return pl.pallas_call(
        functools.partial(pack_kernel, places, len(gains), 16, chips),
        out_shape=(jax.ShapeDtypeStruct((2, half, wide), jnp.bfloat16),) * len(chips),
        in_specs=[SMEM] + [VMEM] * (len(weights) + len(gains)),
        out_specs=(VMEM,) * len(chips),
        compiler_params=pltpu.CompilerParams(vmem_limit_bytes=48 * 2**20),
        name="pack_weights",
    )(spot, *weights, *[gain[:, None] for gain in gains])


def assemble_kernel(shares, extra_at, spot, *refs):
    blocks, mates, whole = refs[: len(shares)], refs[len(shares)], refs[len(shares) + 1]
    rows = blocks[0].shape[1]
    passed = 0
    for (chip, share, other), block in zip(shares, blocks):
        part = rows // share
        for core in range(2):
            first = (spot[0] ^ (2 * chip + core)) * rows
            if share > 1:
                first = first + (spot[1] ^ other) * part
            at = pl.ds(pl.multiple_of(first, 16), part)
            whole[at, :] = mates[passed : passed + part, :] if core else block[0]
        passed += part
    if extra_at is not None:
        gains = refs[-1]
        first = extra_at // LANES * LANES
        for index in range(whole.shape[0] // LANES):
            at = pl.ds(index * LANES, LANES)
            part = whole[at, first : first + LANES].astype(jnp.float32).T
            gains[:, at] = pltpu.roll(part, LANES - extra_at % LANES, 0)[:8]


def assemble(pairs, shares, spot, extra_at):
    mates = swap_core(jnp.concatenate([pair[1] for pair in pairs], axis=0))
    rows, wide = pairs[0].shape[1:]
    shape = (2 * mates.shape[0], wide)
    out_shape = (jax.ShapeDtypeStruct(shape, jnp.bfloat16),)
    if extra_at is not None:
        out_shape += (jax.ShapeDtypeStruct((8, shape[0]), jnp.float32),)
    own = lambda pair: pl.BlockSpec((1,) + pair.shape[1:], lambda i: (0, 0, 0))
    full = lambda *shape: pl.BlockSpec(shape, lambda i: (0,) * len(shape))
    return pl.pallas_call(
        functools.partial(assemble_kernel, shares, extra_at),
        grid=(1,),
        out_shape=out_shape,
        in_specs=[SMEM] + [own(pair) for pair in pairs] + [full(*mates.shape)],
        out_specs=tuple(full(*o.shape) for o in out_shape),
        compiler_params=pltpu.CompilerParams(vmem_limit_bytes=56 * 2**20),
        name="assemble_weights",
    )(spot, *pairs, mates)


def after(values, *earlier):
    anywhere = pl.BlockSpec(memory_space=pl.ANY)
    return pl.pallas_call(
        lambda *refs: None,
        out_shape=tuple(jax.ShapeDtypeStruct(v.shape, v.dtype) for v in values),
        in_specs=[anywhere] * (len(values) + len(earlier)),
        out_specs=(anywhere,) * len(values),
        input_output_aliases={i: i for i in range(len(values))},
        name="after",
    )(*values, *earlier)


def product_kernel(first, index, x, y, *refs):
    out, total = refs[-2:]
    step = pl.program_id(0)

    @pl.when(step == 0)
    def _():
        total[...] = jnp.zeros_like(total)

    total[...] += lax.dot_general(
        x[:, first : first + total.shape[0]], y[...], (((0,), (0,)), ((), ())),
        preferred_element_type=jnp.float32,
    )

    @pl.when(step == pl.num_programs(0) - 1)
    def _():
        out[...] = total[: out.shape[0], :].astype(jnp.bfloat16)


def product(x, y, block, index, first, size, waits):
    rows, wide = y.shape
    step = rows // 4
    held = pad_lanes(size)
    return pl.pallas_call(
        functools.partial(product_kernel, first),
        grid_spec=pltpu.PrefetchScalarGridSpec(
            num_scalar_prefetch=1,
            grid=(4,),
            in_specs=[
                pl.BlockSpec((step, block), lambda k, at: (k, at[0])),
                pl.BlockSpec((step, wide), lambda k, at: (k, 0)),
            ]
            + [pl.BlockSpec(memory_space=pl.ANY)] * len(waits),
            out_specs=pl.BlockSpec((size, wide), lambda k, at: (0, 0)),
            scratch_shapes=[pltpu.VMEM((held, wide), jnp.float32)],
        ),
        out_shape=jax.ShapeDtypeStruct((size, wide), jnp.bfloat16),
        compiler_params=pltpu.CompilerParams(vmem_limit_bytes=48 * 2**20),
        cost_estimate=LITTLE,
        name="product",
    )(index, x, y, *waits)


def spread_kernel(places, count, me, *refs):
    blocks = refs[:count]
    weights = refs[count : count + len(places)]
    outs = refs[count + len(places) : count + 2 * len(places)]
    gain, held = refs[count + 2 * len(places) :]
    for way in range(count):
        held[me[0] ^ way] = blocks[way][...].astype(jnp.float32)
    for out in outs:
        out[...] = jnp.zeros_like(out)
    total = jnp.zeros(gain.shape, jnp.float32)
    for (size, at), weight, out in zip(places, weights, outs):
        full = out.shape[1]
        for index in range(count):
            start = index * size
            span = min(pad_lanes(size + start % LANES), full)
            aligned = min(start // LANES * LANES, full - span)
            shift = start - aligned
            low_lane = at // LANES * LANES
            width = pad_lanes(at - low_lane + size)
            values = held[index][:, low_lane : low_lane + width]
            lane = lax.broadcasted_iota(jnp.int32, values.shape, 1)
            inside = (lane >= at - low_lane) & (lane < at - low_lane + size)
            values = jnp.where(inside, values, 0.0)
            reach = max(span, width)
            if reach > width:
                filling = jnp.zeros((values.shape[0], reach - width), values.dtype)
                values = jnp.concatenate([values, filling], axis=1)
            turned = (shift - (at - low_lane)) % reach
            values = (pltpu.roll(values, turned, 1) if turned else values)[:, :span]
            out[:, aligned : aligned + span] += values
        product = out[...] * weight[...].astype(jnp.float32)
        total = total + jnp.sum(product, axis=1, keepdims=True)
    gain[...] = total


def spread(blocks, weights, me, places, step):
    count = len(blocks)
    rows, wide = weights[0].shape[0], blocks[0].shape[1]
    tile = lambda width: pl.BlockSpec((step, width), lambda i, at: (i, 0))
    block = pl.BlockSpec((step, wide), lambda i, at: (at[0] % 2 * (rows // step) + i, 0))
    return pl.pallas_call(
        functools.partial(spread_kernel, places, count),
        grid_spec=pltpu.PrefetchScalarGridSpec(
            num_scalar_prefetch=1,
            grid=(rows // step,),
            in_specs=[block] * count + [tile(w.shape[1]) for w in weights],
            out_specs=tuple(tile(w.shape[1]) for w in weights) + (tile(1),),
            scratch_shapes=[pltpu.VMEM((count, step, wide), jnp.float32)],
        ),
        out_shape=tuple(jax.ShapeDtypeStruct(w.shape, jnp.float32) for w in weights)
        + (jax.ShapeDtypeStruct((rows, 1), jnp.float32),),
        compiler_params=pltpu.CompilerParams(vmem_limit_bytes=56 * 2**20),
        name="spread_gradients",
    )(me[None].astype(jnp.int32), *blocks, *weights)


def wait(value, *earlier):
    return after((value,), *earlier)[0]


def mark_kernel(*refs):
    refs[-1][...] = jnp.zeros_like(refs[-1])


def flush(*earlier):
    token = pl.pallas_call(
        mark_kernel,
        out_shape=jax.ShapeDtypeStruct((16, LANES), jnp.bfloat16),
        in_specs=[pl.BlockSpec(memory_space=pl.ANY)] * len(earlier),
        out_specs=VMEM,
        name="mark",
    )(*earlier)
    return swap_core(token)


def normed(values):
    inverse = lax.rsqrt(jnp.mean(values * values, axis=-1, keepdims=True) + epsilon)
    return (values * inverse, inverse)


def norm_back(upward, unit_rows, inverse):
    return inverse * (upward - unit_rows * jnp.mean(upward * unit_rows, axis=-1, keepdims=True))


def layout(starts, slot_count):
    slot_index = lax.iota(jnp.int32, slot_count)
    segment_ids = lax.iota(jnp.int32, SEGS)
    segment_len = jnp.where(segment_ids == 0, TRUNK, TILE)
    inside = (slot_index[None, :] >= starts[:, None]) & (
        slot_index[None, :] < (starts + segment_len)[:, None]
    )
    return jnp.any(inside, axis=0)


def dot(left, right):
    return jnp.dot(left, right, preferred_element_type=jnp.float32)


def transpose_dot(left, right):
    return lax.dot_general(
        left, right, (((1,), (1,)), ((), ())), preferred_element_type=jnp.float32
    )


def rows_dot(left, right):
    return lax.dot_general(
        left, right, (((0,), (0,)), ((), ())), preferred_element_type=jnp.float32
    )


def low(values):
    return values.astype(jnp.bfloat16)


def plain(count):
    return count != 8 or lax.axis_size("replica") != 4


def gather_order(count):
    if plain(count):
        return [list(range(count))] * count
    ways = ((0, 1, 2, 3, 5, 4, 6, 7), (0, 1, 4, 5, 3, 2, 6, 7))
    return [[index ^ way for way in ways[index % 2]] for index in range(count)]


def swap_core(values):
    return lax.ppermute(values, "slot", [(i, i ^ 1) for i in range(8)])


def swap_near(values):
    return lax.ppermute(values, "slot", [(i, i ^ (4 if i % 2 else 2)) for i in range(8)])


def swap_far(values):
    return lax.ppermute(values, "slot", [(i, i ^ (2 if i % 2 else 4)) for i in range(8)])


def gather(own):
    count = lax.axis_size("slot")
    if plain(count):
        return jnp.split(lax.all_gather(own, "slot", axis=0, tiled=True), 4, axis=0)
    block = own.shape[0]
    chip = jnp.concatenate([own, swap_core(own)], axis=0)
    near = swap_near(chip)
    corner = swap_far(near[:block])
    return [chip, near, swap_core(near), jnp.concatenate([corner, swap_core(corner)], axis=0)]


def scatter(parts, *between):
    count = lax.axis_size("slot")
    if plain(count):
        whole = jnp.concatenate(parts, axis=0)
        return lax.psum_scatter(whole, "slot", scatter_dimension=0, tiled=True).astype(
            jnp.float32
        )
    chip, near, side, corner = parts
    block = chip.shape[0] // 2
    wide = lambda values: values.astype(jnp.float32)
    near_sum = low(wide(near) + wide(swap_core(side)))
    corner_sum = low(wide(corner[:block]) + wide(swap_core(corner[block:])))
    arrived = swap_far(corner_sum), swap_near(near_sum[block:])
    if between:
        arrived = after(arrived, *between[0](corner_sum))
    near_own = low(wide(near_sum[:block]) + wide(arrived[0]))
    other = low(wide(chip[block:]) + wide(arrived[1]))
    arrived = swap_near(near_own), swap_core(other)
    if between:
        arrived = after(arrived, *between[1](near_own))
    return wide(chip[:block]) + wide(arrived[0]) + wide(arrived[1])


def send(block, way):
    count = lax.axis_size("slot")
    if way == 0:
        return block
    return lax.ppermute(block, "slot", [(i, i ^ way) for i in range(count)])


def sum_trees(part):
    return lax.psum(part, "replica")


def plain_columns(weights, gains, places, wide, heads_in):
    count = lax.axis_size("slot")
    extra_at = sum(size for size, _ in places)
    blocks = jnp.zeros((count, weights[0].shape[0], wide), jnp.bfloat16)
    for weight, (size, at), heads in zip(weights, places, heads_in):
        blocks = blocks.at[:, :, at : at + size].set(split_columns(weight, count, heads))
    for index, gain in enumerate(gains):
        blocks = blocks.at[:, :, extra_at + index].set(gain[None])
    whole = lax.all_to_all(blocks, "slot", 0, 0).reshape(-1, wide)
    return whole, whole[:, extra_at : extra_at + len(gains)].T.astype(jnp.float32)


def send_pairs(pairs):
    return [send(pair, 2 * chip) for chip, pair in enumerate(pairs)]


def swap_halves(pairs):
    trees = lax.axis_size("replica")
    return lax.ppermute(pairs, "replica", [(i, i ^ 1) for i in range(trees)])


def plain_rows(gradient, weights, places, heads_in):
    count = lax.axis_size("slot")
    rows = gradient.shape[0] // count
    blocks = lax.all_to_all(gradient.reshape(count, rows, -1), "slot", 0, 0)
    blocks = sum_trees(blocks).astype(jnp.float32)
    parts = [
        join_columns(blocks[:, :, at : at + size], heads)
        for (size, at), heads in zip(places, heads_in)
    ]
    products = [jnp.sum(p * w.astype(jnp.float32), axis=1) for p, w in zip(parts, weights)]
    return parts, sum(products)


def split_columns(weight, count, heads_in=None):
    rows, columns = weight.shape
    if heads_in is not None and heads_in < count:
        weight = weight.reshape(rows, heads_in, columns // heads_in)
        weight = jnp.repeat(weight, count // heads_in, axis=1)
    else:
        weight = weight.reshape(rows, count, columns // count)
    return weight.transpose(1, 0, 2)


def join_columns(blocks, heads_in=None):
    count, rows, columns = blocks.shape
    if heads_in is not None and heads_in < count:
        blocks = jnp.sum(blocks.reshape(heads_in, count // heads_in, rows, columns), axis=1)
        count = heads_in
    return blocks.transpose(1, 0, 2).reshape(rows, count * columns)


def shards(
    layer_in,
    seg_starts,
    seg_parents,
    w_query,
    w_key,
    w_value,
    w_out,
    w_gate,
    w_up,
    w_down,
    gain_attn,
    gain_ffn,
    out_cotangent,
):
    count = lax.axis_size("slot")
    me = lax.axis_index("slot")
    row_count = layer_in.shape[1]
    slot_count = row_count * count
    features = layer_in.shape[2]
    kv_heads = w_key.shape[1] // HEAD_DIM
    q_width = w_query.shape[1] // count
    heads_width = q_width + 2 * HEAD_DIM
    heads_wide = pad_lanes(heads_width + 2)
    hidden = w_down.shape[0]
    hidden_wide = pad_lanes(hidden)
    starts, parents = seg_starts[0], seg_parents[0]
    tile_starts = jnp.concatenate([lax.iota(jnp.int32, TRUNK_TILES) * TILE, starts[1:]])
    order = jnp.asarray(gather_order(count), jnp.int32)[me]
    tables = turn_tables()
    live = layout(starts, slot_count).astype(jnp.float32).reshape(count, row_count)
    my_live = live[me]

    def cut(values):
        return jnp.split(values, 4, axis=0)

    def blocks_of(parts):
        return jnp.concatenate(parts, axis=0).reshape(count, row_count, parts[0].shape[-1])

    special = not plain(count)
    head_weights = (w_query, w_key, w_value)
    head_places = ((q_width, 0), (HEAD_DIM, q_width), (HEAD_DIM, q_width + HEAD_DIM))
    head_counts = (None, kv_heads, kv_heads)
    hidden_places = ((hidden, 0), (hidden, hidden_wide))
    gain_pair = (gain_attn, gain_ffn)

    def attn_part(part):
        return low(normed(part.astype(jnp.float32))[0] * full_gain_attn)

    if special:
        flat = jnp.stack([me, jnp.zeros_like(me)]).astype(jnp.int32)
        chip = jnp.concatenate([layer_in[0], swap_core(layer_in[0])], axis=0)
        near = swap_near(chip)
        spot = jnp.stack([me, lax.axis_index("replica") % 2]).astype(jnp.int32)
        chips = (0, 1, 2, 3)
        packed = pack(head_weights, gain_pair, flat, head_places, heads_wide, chips, 1)
        hidden_weights = (w_gate, w_up)
        hidden_packed = pack(hidden_weights, (), flat, hidden_places, 2 * hidden_wide, chips[:3], 1)
        hidden_packed += pack(hidden_weights, (), spot, hidden_places, 2 * hidden_wide, chips[3:], 2)
        head_pairs = send_pairs(packed)
        head_pairs = after(head_pairs, flush(hidden_packed[0]))
        whole_shares = tuple((chip, 1, 0) for chip in chips)
        w_heads, gains = assemble(head_pairs, whole_shares, flat, heads_width)
        full_gain_attn, full_gain_ffn = gains[0], gains[1]
        near = wait(near, head_pairs[1])
        corner, side = swap_far(near[:row_count]), swap_core(near)
        hidden_pairs = send_pairs(after(hidden_packed, near))
        token = flush(near)
        attn_parts = [attn_part(part) for part in (wait(chip, token), near, side)]
        parts = [dot(part, w_heads) for part in attn_parts]
        corner = jnp.concatenate([corner, swap_core(corner)], axis=0)
        attn_parts.append(attn_part(corner))
        parts.append(dot(attn_parts[3], w_heads))
        qkv = blocks_of(parts)
    else:
        layer_parts = gather(layer_in[0])
        w_heads, gains = plain_columns(
            head_weights, gain_pair, head_places, heads_wide, head_counts
        )
        w_hidden, _ = plain_columns(
            (w_gate, w_up), (), hidden_places, 2 * hidden_wide, (None, None)
        )
        full_gain_attn, full_gain_ffn = gains[0], gains[1]
        attn_parts = [attn_part(part) for part in layer_parts]
        qkv = blocks_of([dot(part, w_heads) for part in attn_parts])
    attended, *kept = attend_forward(q_width // HEAD_DIM, qkv, tables, tile_starts, parents, order)
    attended = attended.reshape(slot_count, q_width)
    if special:
        hidden_pairs = after(hidden_pairs, attended)
        hidden_pairs += (swap_halves(hidden_pairs[3]),)
        attended = wait(attended, hidden_pairs[3])
    residual = layer_in[0].astype(jnp.float32)
    middle = residual + scatter([low(dot(part, w_out)) for part in cut(attended)])

    w_lower = jnp.pad(w_down, ((0, hidden_wide - hidden), (0, 0)))
    live_rows = jnp.broadcast_to(live.reshape(slot_count, 1), (slot_count, LANES))
    unit_ffn, rms_ffn = normed(middle)
    ffn_input = low(unit_ffn * full_gain_ffn)
    if special:
        feed = lambda index, part, down, held: dense(
            index, order, part, down, live_rows, w_hidden, w_lower, held
        )
        hidden_shares = whole_shares[:3] + ((3, 2, 0), (3, 2, 1))
        (w_hidden,) = assemble(hidden_pairs, hidden_shares, spot, None)
        cotangent = wait(out_cotangent[0], attended)
        chip_down = jnp.concatenate([cotangent, swap_core(cotangent)], axis=0)
        near_down = swap_near(chip_down)
        chip_part = jnp.concatenate([ffn_input, swap_core(ffn_input)], axis=0)
        near_part = swap_near(chip_part)
        chip_back, chip_out, held = feed(0, chip_part, chip_down, ())
        near_down = wait(near_down, chip_back)
        near_part = wait(near_part, near_down)
        corner, corner_down = swap_far(near_part[:row_count]), swap_far(near_down[:row_count])
        side_part, side_down = swap_core(near_part), swap_core(near_down)
        near_back, near_out, held = feed(1, near_part, near_down, held)
        side_back, side_out, held = feed(2, side_part, side_down, held)
        corner, corner_down = after((corner, corner_down), near_back)
        corner_part = jnp.concatenate([corner, swap_core(corner)], axis=0)
        corner_down = jnp.concatenate([corner_down, swap_core(corner_down)], axis=0)
        corner_back, corner_out, held = feed(3, corner_part, corner_down, held)
        back_parts = [chip_back, near_back, side_back, corner_back]
        out_parts = [chip_out, near_out, side_out, corner_out]
    else:
        held, back_parts, out_parts = (), [], []
        pairs = zip(gather(ffn_input), gather(out_cotangent[0]))
        for index, (part, down) in enumerate(pairs):
            back, out, held = dense(
                index, lax.iota(jnp.int32, 4), part, down, live_rows, w_hidden, w_lower, held
            )
            back_parts.append(back)
            out_parts.append(out)
    ffn_rows, down_rows, active_rows, hidden_rows = held
    upstream = out_cotangent[0].astype(jnp.float32) * my_live[:, None]

    def middle_of(ffn_input_grad):
        return upstream + norm_back(ffn_input_grad * full_gain_ffn, unit_ffn, rms_ffn)

    def hidden_part(chip, *waits):
        span = 2 * features // count
        index = ((me ^ chip) // 2)[None].astype(jnp.int32)
        return product(ffn_rows, hidden_rows, span, index, 0, span, waits)

    def to_heads(part):
        return low(transpose_dot(part, w_out))

    def proj_part():
        return low(sum(rows_dot(a, b) for a, b in zip(cut(attended), branch_parts)))

    def heads_part():
        return low(sum(rows_dot(a, b) for a, b in zip(attn_parts, head_parts)))

    if special:
        hidden_parts = []

        def all_hidden(mark):
            for chip in (0, 2, 4, 6):
                hidden_parts.append(hidden_part(chip, mark, *hidden_parts[-1:]))
            return hidden_parts[-1:]

        ffn_input_grad = scatter(back_parts, all_hidden, lambda mark: (mark,))
        middle_grad = middle_of(ffn_input_grad)
        branch = low(middle_grad)
        chip_part = jnp.concatenate([branch, swap_core(branch)], axis=0)
        near_part = swap_near(chip_part)
        hidden_sums = lax.psum(after(hidden_parts, branch), "replica")
        side_part = swap_core(near_part)
        corner = swap_far(near_part[:row_count])
        index = jnp.zeros((1,), jnp.int32)
        grad_down = product(active_rows, down_rows, hidden_wide, index, 0, hidden, (chip_part,))
        corner = wait(corner, grad_down)
        corner_part = jnp.concatenate([corner, swap_core(corner)], axis=0)
        branch_parts = [chip_part, near_part, side_part, corner_part]
    else:
        middle_grad = middle_of(scatter(back_parts))
        branch_parts = gather(low(middle_grad))
    attended_grad = blocks_of([to_heads(part) for part in branch_parts])
    head_grads = attend_backward(attended_grad, kept, tables, tile_starts, parents, order)
    head_parts = cut(head_grads.reshape(slot_count, heads_wide))
    input_parts = [low(transpose_dot(part, w_heads)) for part in head_parts]
    attn_input_grad = scatter(input_parts)
    unit_attn, rms_attn = normed(residual)
    grad_in = low(
        middle_grad + norm_back(attn_input_grad * full_gain_attn, unit_attn, rms_attn)
    )
    grad_proj, grad_heads = proj_part(), heads_part()
    if special:
        out_parts = after(out_parts, grad_in)
    layer_out = low(middle + scatter(out_parts))

    if special:

        def settled(sums):
            blocks = []
            for chip, summed in zip(range(0, count, 2), sums):
                block = send(summed, chip)
                blocks += [block, swap_core(block)]
            return blocks

        hidden_sums = after(hidden_sums, grad_in, grad_heads, grad_proj)
        grad_heads, grad_proj = after((grad_heads, grad_proj), *hidden_sums)
        grad_heads, grad_proj = lax.psum((grad_heads, grad_proj), "replica")
        blocks = settled(hidden_sums)
        grad_gate, grad_up, gain_ffn_sum = spread(blocks, (w_gate, w_up), me, hidden_places, 32)
        grad_heads, grad_proj = after((grad_heads, grad_proj), grad_gate)
        grad_down = lax.psum(wait(grad_down, grad_heads), "replica")
        span = 2 * features // count
        blocks = settled(
            [
                lax.dynamic_slice_in_dim(grad_heads, (me ^ chip) // 2 * span, span)
                for chip in range(0, count, 2)
            ]
        )
        grad_query, grad_key, grad_value, gain_attn_sum = spread(
            blocks, head_weights, me, head_places, 64
        )
        gain_ffn_sum, gain_attn_sum = gain_ffn_sum[:, 0], gain_attn_sum[:, 0]
        grad_down = wait(grad_down, grad_query)
    else:
        grad_down = sum_trees(low(rows_dot(active_rows, down_rows)[:hidden]))
        (grad_gate, grad_up), gain_ffn_sum = plain_rows(
            low(rows_dot(ffn_rows, hidden_rows)), (w_gate, w_up), hidden_places, (None, None)
        )
        grad_proj = sum_trees(grad_proj)
        (grad_query, grad_key, grad_value), gain_attn_sum = plain_rows(
            grad_heads, head_weights, head_places, head_counts
        )
    return (
        layer_out[None],
        grad_in[None],
        grad_query,
        grad_key,
        grad_value,
        grad_proj.astype(jnp.float32),
        grad_gate,
        grad_up,
        grad_down.astype(jnp.float32),
        gain_attn_sum / gain_attn.astype(jnp.float32),
        gain_ffn_sum / gain_ffn.astype(jnp.float32),
    )


def solution(mesh):
    tokens, tree, rows, vector = P("replica", "slot", None), P("replica", None), P("slot", None), P("slot")
    in_specs = (tokens, tree, tree) + (rows,) * 7 + (vector, vector, tokens)
    out_specs = (tokens, tokens) + (rows,) * 7 + (vector, vector)
    return jax.shard_map(shards, mesh=mesh, in_specs=in_specs, out_specs=out_specs, check_vma=False)
```
